512 devices in a mesh: img: 32 (over z, y_hi), txt: 16 (over y_lo, x, core).
Axes of the slice: x: 4, y: 4 (y_hi: 2, y_lo: 2; y = y_hi * 2 + y_lo), z: 16, core: 2. Of those that a mesh axis runs over, the one named last changes fastest.
Arguments:
- picture_tiles: bfloat16 [16384, 32, 1152], P(('img', 'txt')), may hold values from -19 to 19
- query_key_product: bfloat16 [1152, 16], replicated, may hold values from -0.1355288 to 0.1355288
- pooling_exit_matrix: bfloat16 [1152, 1152], P(None, 'txt'), may hold values from -0.179722974 to 0.179722974
- caption_embedding: bfloat16 [16384, 1152], P(('txt', 'img')), may hold values from -11 to 11
- caption_head_matrix: bfloat16 [1152, 1152], P(None, 'txt'), may hold values from -0.179722974 to 0.179722974
- matching_caption_index: int32 [16384], P(('img', 'txt')), may hold values from 0 to 16383, as said below
- natural_inverse_coolness: float32 [1], replicated, may hold values from 2 to 2.5
- score_offset: float32 [1], replicated, may hold values from -6 to -2
- objective_adjoint: float32 [1], replicated, may hold values from 20 to 60
Outputs:
- d_patches: bfloat16 [16384, 32, 1152], P(('img', 'txt'))
- d_text: bfloat16 [16384, 1152], P(('txt', 'img'))
The draws below stay inside these ranges and needn't reach their ends.
Inputs may be any that keep to these rules, and one draw needn't show every extreme that they name: `matching_caption_index`: each text is the matching text of exactly one image.
All inputs are finite; a program needn't handle non-finite values.
Results may differ from the reference program's by a relative error of at most 0.024.
Values may be sent and summed in bfloat16 or wider, within the bound.
No kernel may reach another device: no remote copies, remote signals or barrier semaphores. Data moves between devices by JAX's collectives and lax.ppermute only.
A program may use at most 64 MiB of HBM per device.

```python
import jax
import jax.numpy as jnp
from jax import lax

D = 1152
HEADS = 16
PATCHES = 32
BATCH = 16384
IMG_BLOCK = 512
TXT_BLOCK = 1024
N_IMG = 32
N_TXT = 16


def probe_base(key):
    return jnp.clip(jax.random.normal(key, (D, HEADS), jnp.float32), -3.0, 3.0)


def pair_ordering(key):
    return jax.random.permutation(jax.random.fold_in(key, 101), BATCH).astype(jnp.int32)


def pair_vectors(key):
    cluster_count = max(BATCH // 32, 2)
    group_ids = jax.random.randint(jax.random.fold_in(key, 103), (BATCH,), 0, cluster_count)
    centers = jax.random.normal(jax.random.fold_in(key, 107), (cluster_count, D), jnp.float32)
    individual = jax.random.normal(jax.random.fold_in(key, 109), (BATCH, D), jnp.float32)
    return jnp.clip(0.63 * centers[group_ids] + 0.77 * individual, -5.0, 5.0)


def weight_shared(key):
    return jnp.clip(jax.random.normal(jax.random.fold_in(key, 113), (D, D), jnp.float32), -4.5, 4.5)


def draw_query_key_product(key, part):
    probe_rows = probe_base(key)
    return (probe_rows * (1.5 * D ** (-0.5))).astype(jnp.bfloat16)


def draw_matching_caption_index(key, part):
    ordering = pair_ordering(key)
    return ordering


def draw_pooling_exit_matrix(key, part):
    shared = weight_shared(key)
    key = jax.random.fold_in(key, 11)
    single = jnp.clip(jax.random.normal(key, (D, D), jnp.float32), -4.5, 4.5)
    return ((0.89 * shared + 0.45 * single) * D ** (-0.5)).astype(jnp.bfloat16)


def draw_caption_head_matrix(key, part):
    shared = weight_shared(key)
    key = jax.random.fold_in(key, 17)
    single = jnp.clip(jax.random.normal(key, (D, D), jnp.float32), -4.5, 4.5)
    return ((0.89 * shared + 0.45 * single) * D ** (-0.5)).astype(jnp.bfloat16)


def draw_caption_embedding(key, part):
    ordering = pair_ordering(key)
    vectors = pair_vectors(key)
    key = jax.random.fold_in(key, 13)
    noise_key = jax.random.fold_in(key, 0)
    matched = jnp.zeros((BATCH, D), jnp.float32).at[ordering].set(vectors)
    noise_values = jnp.clip(jax.random.normal(noise_key, (BATCH, D), jnp.float32), -4.0, 4.0)
    values = 0.9 * matched + 0.44 * noise_values
    return jnp.clip(values, -11.0, 11.0).astype(jnp.bfloat16)


def draw_picture_tiles(key, part):
    vectors = pair_vectors(key)
    key = jax.random.fold_in(key, 7)
    noise_key = jax.random.fold_in(key, 0)
    common = 0.8 * vectors[:, None, :]
    noise_values = jnp.clip(jax.random.normal(noise_key, (BATCH, PATCHES, D), jnp.float32), -4.0, 4.0)
    values = common + 0.6 * noise_values
    return values.astype(jnp.bfloat16)


def setup_inputs(seed: int = 0) -> dict:
    arg_keys = jax.random.split(jax.random.key(seed), 10)
    picture_tiles = draw_picture_tiles(jax.random.fold_in(arg_keys[9], 71), 0)
    query_key_product = draw_query_key_product(jax.random.fold_in(arg_keys[9], 71), 0)
    pooling_exit_matrix = draw_pooling_exit_matrix(jax.random.fold_in(arg_keys[9], 71), 0)
    caption_embedding = draw_caption_embedding(jax.random.fold_in(arg_keys[9], 71), 0)
    caption_head_matrix = draw_caption_head_matrix(jax.random.fold_in(arg_keys[9], 71), 0)
    matching_caption_index = draw_matching_caption_index(jax.random.fold_in(arg_keys[9], 71), 0)
    natural_inverse_coolness = jnp.clip(jax.random.uniform(arg_keys[6], (1,), jnp.float32, 2.0, 2.5), 2.0, 2.5)
    score_offset = jnp.clip(jax.random.uniform(arg_keys[7], (1,), jnp.float32, -6.0, -2.0), -6.0, -2.0)
    objective_adjoint = jnp.clip(jax.random.uniform(arg_keys[8], (1,), jnp.float32, 20.0, 60.0), 20.0, 60.0)
    return {"picture_tiles": picture_tiles, "query_key_product": query_key_product, "pooling_exit_matrix": pooling_exit_matrix, "caption_embedding": caption_embedding, "caption_head_matrix": caption_head_matrix, "matching_caption_index": matching_caption_index, "natural_inverse_coolness": natural_inverse_coolness, "score_offset": score_offset, "objective_adjoint": objective_adjoint}


EPSILON = 1e-06

def quantized_numbers(values):
    return lax.optimization_barrier(values.astype(jnp.bfloat16)).astype(jnp.float32)

def attention_weights(patch_rows, query_key_product):
    scores = jnp.einsum('bpd,dh->bhp', patch_rows.astype(jnp.float32), query_key_product.astype(jnp.float32))
    return jax.nn.softmax(scores, axis=-1)

def pool_forward(patch_rows, query_key_product):
    attend = attention_weights(patch_rows, query_key_product)
    per_head = patch_rows.reshape(patch_rows.shape[0], PATCHES, HEADS, D // HEADS).astype(jnp.float32)
    pooled = jnp.einsum('bhp,bphc->bhc', quantized_numbers(attend), per_head)
    return pooled.reshape(patch_rows.shape[0], D).astype(jnp.bfloat16)

def pool_backward(patch_rows, query_key_product, dpooled):
    attend = attention_weights(patch_rows, query_key_product)
    attend_low = quantized_numbers(attend)
    per_head = patch_rows.reshape(patch_rows.shape[0], PATCHES, HEADS, D // HEADS).astype(jnp.float32)
    dpooled_low = quantized_numbers(dpooled).reshape(patch_rows.shape[0], HEADS, D // HEADS)
    dattend = jnp.einsum('bhc,bphc->bhp', dpooled_low, per_head)
    dscores = attend * (dattend - lax.optimization_barrier(jnp.sum(attend * dattend, axis=-1, keepdims=True)))
    direct = jnp.einsum('bhp,bhc->bphc', attend_low, dpooled_low).reshape(patch_rows.shape[0], PATCHES, D)
    through = jnp.einsum('bhp,dh->bpd', quantized_numbers(dscores), query_key_product.astype(jnp.float32))
    return (direct + through).astype(jnp.bfloat16)

def inverse_norm(pre_rows):
    return lax.rsqrt(lax.optimization_barrier(jnp.sum(pre_rows * pre_rows, axis=-1, keepdims=True)) + EPSILON)

def reference(picture_tiles, query_key_product, pooling_exit_matrix, caption_embedding, caption_head_matrix, matching_caption_index, natural_inverse_coolness, score_offset, objective_adjoint):
    image_groups = picture_tiles.reshape(N_IMG, IMG_BLOCK, PATCHES, D)
    pooled = lax.map(lambda patch_rows: pool_forward(patch_rows, query_key_product), image_groups).reshape(BATCH, D)
    image_pre = jnp.dot(pooled, pooling_exit_matrix, preferred_element_type=jnp.float32)
    text_pre = jnp.dot(caption_embedding, caption_head_matrix, preferred_element_type=jnp.float32)
    image_inv = inverse_norm(image_pre)
    text_inv = inverse_norm(text_pre)
    image_unit = (image_pre * image_inv).astype(jnp.bfloat16)
    text_unit = (text_pre * text_inv).astype(jnp.bfloat16)
    score_coolness = jnp.exp(natural_inverse_coolness[0])
    collected_captions = text_unit.astype(jnp.float32)
    columns = jnp.arange(BATCH, dtype=jnp.int32)

    def tile_step(text_total, inputs):
        row_block, positives = inputs
        line_elements = row_block.astype(jnp.float32)
        couple_scores = score_coolness * jnp.dot(line_elements, collected_captions.T, precision=lax.Precision.HIGHEST) + score_offset[0]
        match_polarity = jnp.where(positives[:, None] == columns[None, :], 1.0, -1.0).astype(couple_scores.dtype)
        score_derivative = -objective_adjoint[0] * match_polarity * jax.nn.sigmoid(-match_polarity * couple_scores)
        scaled_couples = quantized_numbers(score_coolness * score_derivative)
        image_part = jnp.einsum('ikj,kjd->ikd', scaled_couples.reshape(IMG_BLOCK, N_TXT, TXT_BLOCK), collected_captions.reshape(N_TXT, TXT_BLOCK, D), precision=lax.Precision.HIGHEST)
        image_rows = lax.optimization_barrier(jnp.sum(quantized_numbers(image_part), axis=1))
        text_part = jnp.dot(scaled_couples.T, line_elements, precision=lax.Precision.HIGHEST)
        return (text_total + quantized_numbers(text_part), image_rows)
    text_grad, image_rows = lax.scan(tile_step, jnp.zeros((BATCH, D), jnp.float32), (image_unit.reshape(N_IMG, IMG_BLOCK, D), matching_caption_index.reshape(N_IMG, IMG_BLOCK)))
    image_grad = image_rows.reshape(BATCH, D)
    image_dpre = (image_inv * image_grad - image_inv ** 3 * image_pre * lax.optimization_barrier(jnp.sum(image_pre * image_grad, axis=-1, keepdims=True))).astype(jnp.bfloat16)
    text_dpre = (text_inv * text_grad - text_inv ** 3 * text_pre * lax.optimization_barrier(jnp.sum(text_pre * text_grad, axis=-1, keepdims=True))).astype(jnp.bfloat16)
    dpooled = jnp.dot(image_dpre, pooling_exit_matrix.T, preferred_element_type=jnp.float32)
    d_text = jnp.dot(text_dpre, caption_head_matrix.T, preferred_element_type=jnp.float32).astype(jnp.bfloat16)
    d_patches = lax.map(lambda pair: pool_backward(pair[0], query_key_product, pair[1]), (image_groups, dpooled.reshape(N_IMG, IMG_BLOCK, D))).reshape(BATCH, PATCHES, D)
    return (d_patches, d_text)
```

```python
import jax
import jax.numpy as jnp
from jax import lax
from jax.experimental import pallas as pl
from jax.experimental.pallas import tpu as pltpu
from jax.sharding import Mesh, PartitionSpec as P

EPSILON = 1e-06
INTERPRET = False
BF, F32 = jnp.bfloat16, jnp.float32
NZ, NYH, NYL, NX, NC = 16, 2, 2, 4, 2
Y = ("y_hi", "y_lo")
XY = ("y_hi", "y_lo", "x")
VMEM = pltpu.VMEM
SMEM = pltpu.SMEM
NEAR = (0, 3, -3, 6, -6)
TEXT_OFFSETS = NEAR + tuple(o + 1 for o in NEAR) + tuple(o - 1 for o in NEAR) + (8,)


def take_from(values, axis, distance, size):
    return lax.ppermute(values, axis, [((i + distance) % size, i) for i in range(size)])


def swap_cores(values):
    return lax.ppermute(values, "core", [(0, 1), (1, 0)])


def nt_dot(a, b):
    return lax.dot_general(a, b, (((1,), (1,)), ((), ())), preferred_element_type=F32)


def tn_dot(a, b):
    return lax.dot_general(a, b, (((0,), (0,)), ((), ())), preferred_element_type=F32)


def nn_dot(a, b):
    return jnp.dot(a, b, preferred_element_type=F32)


def call(kernel, out_shape, *, flops=0, transcendentals=0, moved=0, **kw):
    return pl.pallas_call(
        kernel,
        out_shape=out_shape,
        compiler_params=pltpu.CompilerParams(vmem_limit_bytes=40 * 1024 * 1024),
        cost_estimate=pl.CostEstimate(
            flops=flops, transcendentals=transcendentals, bytes_accessed=moved
        ),
        interpret=INTERPRET,
        **kw,
    )


def attention_forward(tiles, query_key, spread, patches):
    rows, width = tiles.shape
    heads = query_key.shape[1]
    images = rows // patches
    step = min(8, images)

    def kernel(tile_ref, qk_ref, spread_ref, attend_ref, pooled_ref):
        tile = tile_ref[...]
        scores = nn_dot(tile, qk_ref[...]).reshape(step, patches, heads)
        top = jnp.max(scores, axis=1, keepdims=True)
        raised = jnp.exp(scores - top)
        attend = raised / jnp.sum(raised, axis=1, keepdims=True)
        attend = attend.reshape(step * patches, heads)
        attend_ref[...] = attend
        wide = nn_dot(attend.astype(BF), spread_ref[...])
        mixed = (wide * tile.astype(F32)).reshape(step, patches, width)
        pooled_ref[...] = jnp.sum(mixed, axis=1)

    return call(
        kernel,
        (
            jax.ShapeDtypeStruct((rows, heads), F32),
            jax.ShapeDtypeStruct((images, width), F32),
        ),
        grid=(images // step,),
        in_specs=[
            pl.BlockSpec((step * patches, width), lambda i: (i, 0)),
            pl.BlockSpec((width, heads), lambda i: (0, 0)),
            pl.BlockSpec((heads, width), lambda i: (0, 0)),
        ],
        out_specs=[
            pl.BlockSpec((step * patches, heads), lambda i: (i, 0)),
            pl.BlockSpec((step, width), lambda i: (i, 0)),
        ],
        flops=4 * rows * width * 128,
        moved=rows * width * 2,
    )(tiles, query_key, spread)


def attention_backward(tiles, attend, dpooled, query_key_t, spread, gather, patches):
    rows, width = tiles.shape
    heads = attend.shape[1]
    images = rows // patches
    step = min(8, images)

    def kernel(tile_ref, attend_ref, dpooled_ref, qkt_ref, spread_ref, gather_ref, out_ref):
        block = step * patches
        upstream = dpooled_ref[...]
        upstream = jnp.broadcast_to(upstream[:, None, :], (step, patches, width))
        upstream = upstream.reshape(block, width)
        product = tile_ref[...].astype(F32) * upstream
        high = product.astype(BF)
        low = (product - high.astype(F32)).astype(BF)
        dattend = nn_dot(high, gather_ref[...]) + nn_dot(low, gather_ref[...])
        attend = attend_ref[...]
        weighted = (attend * dattend).reshape(step, patches, heads)
        mean = jnp.broadcast_to(
            jnp.sum(weighted, axis=1, keepdims=True), (step, patches, heads)
        ).reshape(block, heads)
        dscores = attend * (dattend - mean)
        direct = nn_dot(attend.astype(BF), spread_ref[...]) * upstream
        through = nn_dot(dscores.astype(BF), qkt_ref[...])
        out_ref[...] = (direct + through).astype(BF)

    return call(
        kernel,
        jax.ShapeDtypeStruct((rows, width), BF),
        grid=(images // step,),
        in_specs=[
            pl.BlockSpec((step * patches, width), lambda i: (i, 0)),
            pl.BlockSpec((step * patches, heads), lambda i: (i, 0)),
            pl.BlockSpec((step, width), lambda i: (i, 0)),
            pl.BlockSpec((heads, width), lambda i: (0, 0)),
            pl.BlockSpec((heads, width), lambda i: (0, 0)),
            pl.BlockSpec((width, heads), lambda i: (0, 0)),
        ],
        out_specs=pl.BlockSpec((step * patches, width), lambda i: (i, 0)),
        flops=8 * rows * width * 128,
        moved=rows * width * 4,
    )(tiles, attend, dpooled, query_key_t, spread, gather)


def to_common(blocks, place):
    x, y_lo, core = place
    b = [[[blocks[(c * 2 + dy) * 4 + dx] for dx in range(4)] for dy in range(2)] for c in range(2)]
    b = [[[jnp.where(core == 0, b[c][dy][dx], b[1 - c][dy][dx]) for dx in range(4)] for dy in range(2)] for c in range(2)]
    b = [[[jnp.where(y_lo == 0, b[c][y][dx], b[c][1 - y][dx]) for dx in range(4)] for y in range(2)] for c in range(2)]
    for bit in (1, 2):
        moved = (x & bit) != 0
        b = [[[jnp.where(moved, b[c][y][(k - bit) % 4], b[c][y][k]) for k in range(4)] for y in range(2)] for c in range(2)]
    return [b[c][y][k] for c in range(2) for y in range(2) for k in range(4)]


def from_common(blocks, place):
    x, y_lo, core = place
    b = [[[blocks[(c * 2 + y) * 4 + k] for k in range(4)] for y in range(2)] for c in range(2)]
    for bit in (1, 2):
        moved = (x & bit) != 0
        b = [[[jnp.where(moved, b[c][y][(k + bit) % 4], b[c][y][k]) for k in range(4)] for y in range(2)] for c in range(2)]
    b = [[[jnp.where(y_lo == 0, b[c][y][dx], b[c][1 - y][dx]) for dx in range(4)] for y in range(2)] for c in range(2)]
    b = [[[jnp.where(core == 0, b[c][dy][dx], b[1 - c][dy][dx]) for dx in range(4)] for dy in range(2)] for c in range(2)]
    return [b[c][y][k] for c in range(2) for y in range(2) for k in range(4)]


def project(place, rows, own, other):
    count, width = rows.shape
    column = width // 16

    def kernel(place_ref, rows_ref, own_ref, other_ref, pre_ref, unit_ref):
        spot = place_ref[0], place_ref[1], place_ref[2]
        line = rows_ref[...].astype(BF)
        halves = nt_dot(line, own_ref[...]), nt_dot(line, other_ref[...])
        blocks = [half[:, i * column : (i + 1) * column] for half in halves for i in range(8)]
        for i, block in enumerate(to_common(blocks, spot)):
            pre_ref[:, i * column : (i + 1) * column] = block
        pre = pre_ref[...]
        inverse = lax.rsqrt(jnp.sum(pre * pre, axis=-1, keepdims=True) + EPSILON)
        unit_ref[...] = (pre * inverse).astype(BF)

    return call(
        kernel,
        (
            jax.ShapeDtypeStruct((count, width), F32),
            jax.ShapeDtypeStruct((count, width), BF),
        ),
        in_specs=[pl.BlockSpec(memory_space=SMEM)] + [pl.BlockSpec(memory_space=VMEM)] * 3,
        out_specs=[pl.BlockSpec(memory_space=VMEM)] * 2,
        flops=2 * count * width * width,
        moved=2 * width * width,
    )(place, rows, own, other)


def project_back(place, pre, parts, own, other, out_dtype):
    count, width = pre.shape
    column = width // 16

    def kernel(place_ref, pre_ref, *refs):
        part_refs, (own_ref, other_ref, out_ref, kept) = refs[: len(parts)], refs[len(parts) :]
        spot = place_ref[0], place_ref[1], place_ref[2]
        upstream = None
        for ref in part_refs:
            if len(ref.shape) == 3:
                terms = [ref[i].astype(F32) for i in range(ref.shape[0])]
            else:
                terms = [ref[...].astype(F32)]
            for term in terms:
                upstream = term if upstream is None else upstream + term
        pre = pre_ref[...]
        inverse = lax.rsqrt(jnp.sum(pre * pre, axis=-1, keepdims=True) + EPSILON)
        along = jnp.sum(pre * upstream, axis=-1, keepdims=True)
        dpre = inverse * upstream - inverse**3 * pre * along
        blocks = [dpre[:, i * column : (i + 1) * column] for i in range(16)]
        for i, block in enumerate(from_common(blocks, spot)):
            kept[:, i * column : (i + 1) * column] = block
        turned = kept[...].astype(BF)
        half = width // 2
        own_part = nn_dot(turned[:, :half], own_ref[...])
        total = own_part + nn_dot(turned[:, half:], other_ref[...])
        out_ref[...] = total.astype(BF).astype(out_dtype)

    return call(
        kernel,
        jax.ShapeDtypeStruct((count, width), out_dtype),
        in_specs=[pl.BlockSpec(memory_space=SMEM)]
        + [pl.BlockSpec(memory_space=VMEM)] * (3 + len(parts)),
        out_specs=pl.BlockSpec(memory_space=VMEM),
        scratch_shapes=[pltpu.VMEM((count, width), F32)],
        flops=2 * count * width * width,
        moved=2 * width * width,
    )(place, pre, *parts, own, other)


def grid_tile(scalars, texts, text_ids, images, positives, text_sum, cuts):
    text_count, width = texts.shape
    image_count = images.shape[0]
    block = min(256, image_count)
    steps = image_count // block

    def kernel(scalar_ref, texts_ref, ids_ref, images_ref, positives_ref, *refs):
        if text_sum is not None:
            sum_ref, *refs = refs
        image_part_ref, *text_refs = refs
        total = text_refs[-1] if cuts is not None else text_refs[0]
        step = pl.program_id(0)
        coolness, offset, scale = scalar_ref[0], scalar_ref[1], scalar_ref[2]
        texts = texts_ref[...]
        images = images_ref[...]
        logits = coolness * nt_dot(texts, images) + offset
        match = ids_ref[...] == positives_ref[...]
        steep = jnp.where(match, -scale, scale)
        slope = steep / (1.0 + jnp.exp(jnp.where(match, logits, -logits)))
        weighted = slope.astype(BF)
        image_part_ref[...] = tn_dot(weighted, texts).astype(BF)
        term = nn_dot(weighted, images)

        @pl.when(step == 0)
        def _():
            total[...] = term if text_sum is None else sum_ref[...] + term

        @pl.when(step > 0)
        def _():
            total[...] += term

        if cuts is not None:

            @pl.when(step == steps - 1)
            def _():
                start = 0
                for ref, size in zip(text_refs, cuts):
                    ref[...] = total[start : start + size, :].astype(BF)
                    start += size

    whole = pl.BlockSpec((text_count, width), lambda i: (0, 0))
    in_specs = [
        pl.BlockSpec(memory_space=SMEM),
        whole,
        pl.BlockSpec((text_count, 1), lambda i: (0, 0)),
        pl.BlockSpec((block, width), lambda i: (i, 0)),
        pl.BlockSpec((1, block), lambda i: (0, i)),
    ]
    operands = [scalars, texts, text_ids, images, positives]
    if text_sum is not None:
        in_specs.append(whole)
        operands.append(text_sum)
    outs = [jax.ShapeDtypeStruct((image_count, width), BF)]
    out_specs = [pl.BlockSpec((block, width), lambda i: (i, 0))]
    scratch = []
    if cuts is None:
        outs.append(jax.ShapeDtypeStruct((text_count, width), F32))
        out_specs.append(whole)
    else:
        for size in cuts:
            outs.append(jax.ShapeDtypeStruct((size, width), BF))
            out_specs.append(pl.BlockSpec((size, width), lambda i: (0, 0)))
        scratch.append(pltpu.VMEM((text_count, width), F32))
    return call(
        kernel,
        tuple(outs),
        grid=(steps,),
        in_specs=in_specs,
        out_specs=out_specs,
        scratch_shapes=scratch,
        flops=6 * text_count * image_count * width,
        transcendentals=text_count * image_count,
        moved=2 * width * (text_count + 2 * image_count),
    )(*operands)


def gather_matrix(piece):
    column = piece.shape[0]
    cut = column // 2 // 16 * 16
    right = take_from(piece, "x", 1, NX)
    left = take_from(piece, "x", -1, NX)
    far = jnp.concatenate(
        [take_from(right[:cut], "x", 1, NX), take_from(left[cut:], "x", -1, NX)], axis=0
    )
    beside = [
        take_from(piece, Y, 1, 4),
        take_from(right, Y, 1, 4),
        take_from(far, Y, -1, 4),
        take_from(left, Y, -1, 4),
    ]
    own = jnp.concatenate([piece, right, far, left] + beside, axis=0)
    return own, swap_cores(own)


def gather_texts(unit):
    near = jnp.concatenate(
        [unit] + [take_from(unit, "z", distance, NZ) for distance in NEAR[1:]], axis=0
    )
    ahead = take_from(near, "z", 1, NZ)
    behind = take_from(near, "z", -1, NZ)
    count = unit.shape[0]
    far = take_from(near[3 * count : 4 * count], "z", 2, NZ)
    return jnp.concatenate([near, ahead, behind, far], axis=0)


def scatter_texts(near, ahead, behind, far):
    count = far.shape[0]
    total = near.astype(F32) + take_from(ahead, "z", -1, NZ) + take_from(behind, "z", 1, NZ)
    far = take_from(far, "z", -2, NZ)
    parts = []
    for place, distance in enumerate(NEAR):
        part = total[place * count : (place + 1) * count]
        if distance == 6:
            part = part + far
        part = part.astype(BF)
        if distance:
            part = take_from(part, "z", -distance, NZ)
        parts.append(part)
    return parts


def to_all(values):
    spread = jnp.broadcast_to(values[None], (16,) + values.shape)
    return lax.all_to_all(spread, XY, 0, 0, tiled=True)


def shards(
    picture_tiles,
    query_key_product,
    pooling_exit_matrix,
    caption_embedding,
    caption_head_matrix,
    matching_caption_index,
    natural_inverse_coolness,
    score_offset,
    objective_adjoint,
):
    images, patches, width = picture_tiles.shape
    heads = query_key_product.shape[1]
    z, y_hi, y_lo, x, core = (lax.axis_index(a) for a in ("z", "y_hi", "y_lo", "x", "core"))
    place = jnp.stack([x, y_lo, core]).astype(jnp.int32)

    text_own, text_other = gather_matrix(caption_head_matrix.T)
    exit_own, exit_other = gather_matrix(pooling_exit_matrix.T)

    own_positives = to_all(matching_caption_index).reshape(1, -1)
    other_positives = swap_cores(own_positives)

    head_of = jnp.arange(width, dtype=jnp.int32) // (width // heads)
    spread = (head_of[None, :] == jnp.arange(heads, dtype=jnp.int32)[:, None]).astype(BF)
    gather = (head_of[:, None] == jnp.arange(heads, dtype=jnp.int32)[None, :]).astype(BF)
    tiles = picture_tiles.reshape(images * patches, width)
    attend, pooled = attention_forward(tiles, query_key_product, spread, patches)

    text_pre, text_unit = project(place, caption_embedding, text_own, text_other)
    texts = gather_texts(text_unit)
    image_pre, image_unit = project(place, pooled, exit_own, exit_other)
    own_images = to_all(image_unit).reshape(-1, width)
    other_images = swap_cores(own_images)

    txt = (y_lo * NX + x) * NC + core
    count = caption_embedding.shape[0]
    source = (z + jnp.array(TEXT_OFFSETS, jnp.int32)) % NZ
    first = (txt * (NZ * NYH) + source * NYH + y_hi) * count
    text_ids = (first[:, None] + jnp.arange(count, dtype=jnp.int32)[None, :]).reshape(-1, 1)

    coolness = jnp.exp(natural_inverse_coolness[0])
    scalars = jnp.stack([coolness, score_offset[0], coolness * objective_adjoint[0]])
    own_part, text_sum = grid_tile(scalars, texts, text_ids, own_images, own_positives, None, None)
    cuts = (5 * count, 5 * count, 5 * count, count)
    other_part, near, ahead, behind, far = grid_tile(
        scalars, texts, text_ids, other_images, other_positives, text_sum, cuts
    )

    chip_part = (own_part.astype(F32) + swap_cores(other_part).astype(F32)).astype(BF)
    image_parts = lax.all_to_all(chip_part.reshape(16, -1, width), XY, 0, 0, tiled=True)
    text_parts = scatter_texts(near, ahead, behind, far)

    dpooled = project_back(place, image_pre, [image_parts], exit_own, exit_other, F32)
    d_patches = attention_backward(
        tiles, attend, dpooled, query_key_product.T, spread, gather, patches
    )
    d_text = project_back(place, text_pre, text_parts, text_own, text_other, BF)
    return (d_patches.reshape(images, patches, width), d_text)


def solution(mesh):
    chips = Mesh(
        mesh.devices.reshape(NZ, NYH, NYL, NX, NC), ("z", "y_hi", "y_lo", "x", "core")
    )
    img, txt = ("z", "y_hi"), ("y_lo", "x", "core")
    return jax.shard_map(
        shards,
        mesh=chips,
        in_specs=(
            P(img + txt, None, None),
            P(),
            P(None, txt),
            P(txt + img, None),
            P(None, txt),
            P(img + txt),
            P(),
            P(),
            P(),
        ),
        out_specs=(P(img + txt, None, None), P(txt + img, None)),
        check_vma=False,
    )
```

```python
import jax
import jax.numpy as jnp
from jax import lax
from jax.experimental import pallas as pl
from jax.experimental.pallas import tpu as pltpu
from jax.sharding import Mesh, PartitionSpec as P

EPSILON = 1e-06
INTERPRET = False
BF, F32 = jnp.bfloat16, jnp.float32
NZH, NZL, NYH, NYL, NX, NC = 4, 4, 2, 2, 4, 2
NZ = NZH * NZL
Z = ("z_hi", "z_lo")
XY = ("y_hi", "y_lo", "x")
TAIL = 128
VMEM = pltpu.VMEM
SMEM = pltpu.SMEM


def take_from(values, axis, distance, size):
    return lax.ppermute(values, axis, [((i + distance) % size, i) for i in range(size)])


def swap_cores(values):
    return lax.ppermute(values, "core", [(0, 1), (1, 0)])


def nt_dot(a, b):
    return lax.dot_general(a, b, (((1,), (1,)), ((), ())), preferred_element_type=F32)


def tn_dot(a, b):
    return lax.dot_general(a, b, (((0,), (0,)), ((), ())), preferred_element_type=F32)


def nn_dot(a, b):
    return jnp.dot(a, b, preferred_element_type=F32)


def call(kernel, out_shape, *, flops=0, transcendentals=0, moved=0, limit=16, **kw):
    return pl.pallas_call(
        kernel,
        out_shape=out_shape,
        compiler_params=pltpu.CompilerParams(vmem_limit_bytes=limit * 1024 * 1024),
        cost_estimate=pl.CostEstimate(
            flops=flops, transcendentals=transcendentals, bytes_accessed=moved
        ),
        interpret=INTERPRET,
        **kw,
    )


def attention_forward(tiles, query_key, spread, patches):
    rows, width = tiles.shape
    heads = query_key.shape[1]
    images = rows // patches
    step = min(8, images)

    def kernel(tile_ref, qk_ref, spread_ref, attend_ref, pooled_ref):
        tile = tile_ref[...]
        scores = nn_dot(tile, qk_ref[...]).reshape(step, patches, heads)
        top = jnp.max(scores, axis=1, keepdims=True)
        raised = jnp.exp(scores - top)
        attend = raised / jnp.sum(raised, axis=1, keepdims=True)
        attend = attend.reshape(step * patches, heads)
        attend_ref[...] = attend
        wide = nn_dot(attend.astype(BF), spread_ref[...])
        mixed = (wide * tile.astype(F32)).reshape(step, patches, width)
        pooled_ref[...] = jnp.sum(mixed, axis=1)

    return call(
        kernel,
        (
            jax.ShapeDtypeStruct((rows, heads), F32),
            jax.ShapeDtypeStruct((images, width), F32),
        ),
        grid=(images // step,),
        in_specs=[
            pl.BlockSpec((step * patches, width), lambda i: (i, 0)),
            pl.BlockSpec((width, heads), lambda i: (0, 0)),
            pl.BlockSpec((heads, width), lambda i: (0, 0)),
        ],
        out_specs=[
            pl.BlockSpec((step * patches, heads), lambda i: (i, 0)),
            pl.BlockSpec((step, width), lambda i: (i, 0)),
        ],
        flops=4 * rows * width * 128,
        moved=rows * width * 2,
    )(tiles, query_key, spread)


def attention_backward(tiles, attend, dpooled, query_key_t, spread, gather, patches):
    rows, width = tiles.shape
    heads = attend.shape[1]
    images = rows // patches
    step = min(8, images)

    def kernel(tile_ref, attend_ref, dpooled_ref, qkt_ref, spread_ref, gather_ref, out_ref):
        block = step * patches
        upstream = dpooled_ref[...]
        upstream = jnp.broadcast_to(upstream[:, None, :], (step, patches, width))
        upstream = upstream.reshape(block, width)
        product = tile_ref[...].astype(F32) * upstream
        high = product.astype(BF)
        low = (product - high.astype(F32)).astype(BF)
        dattend = nn_dot(high, gather_ref[...]) + nn_dot(low, gather_ref[...])
        attend = attend_ref[...]
        weighted = (attend * dattend).reshape(step, patches, heads)
        mean = jnp.broadcast_to(
            jnp.sum(weighted, axis=1, keepdims=True), (step, patches, heads)
        ).reshape(block, heads)
        dscores = attend * (dattend - mean)
        direct = nn_dot(attend.astype(BF), spread_ref[...]) * upstream
        through = nn_dot(dscores.astype(BF), qkt_ref[...])
        out_ref[...] = (direct + through).astype(BF)

    return call(
        kernel,
        jax.ShapeDtypeStruct((rows, width), BF),
        grid=(images // step,),
        in_specs=[
            pl.BlockSpec((step * patches, width), lambda i: (i, 0)),
            pl.BlockSpec((step * patches, heads), lambda i: (i, 0)),
            pl.BlockSpec((step, width), lambda i: (i, 0)),
            pl.BlockSpec((heads, width), lambda i: (0, 0)),
            pl.BlockSpec((heads, width), lambda i: (0, 0)),
            pl.BlockSpec((width, heads), lambda i: (0, 0)),
        ],
        out_specs=pl.BlockSpec((step * patches, width), lambda i: (i, 0)),
        flops=8 * rows * width * 128,
        moved=rows * width * 4,
    )(tiles, attend, dpooled, query_key_t, spread, gather)


def project(core, rows, matrix, partners=None):
    count, width = rows.shape
    half = width // 2
    tail = 0 if partners is None else TAIL

    def kernel(core_ref, rows_ref, *refs):
        matrix_refs, refs = refs[: len(matrix)], refs[len(matrix) :]
        pre_ref, unit_ref = refs[-2:]
        line = rows_ref[...].astype(BF)
        if len(matrix) == 1:
            pre = nt_dot(line, matrix_refs[0][...])
            pre_ref[...] = pre
        else:
            first = core_ref[0] == 0
            mine, theirs = nt_dot(line, matrix_refs[0][...]), nt_dot(line, matrix_refs[1][...])
            pre_ref[:, :half] = jnp.where(first, mine, theirs)
            pre_ref[:, half:] = jnp.where(first, theirs, mine)
            pre = pre_ref[...]
        inverse = lax.rsqrt(jnp.sum(pre * pre, axis=-1, keepdims=True) + EPSILON)
        unit_ref[:, :width] = (pre * inverse).astype(BF)
        if tail:
            index = refs[0][...]
            lane = lax.broadcasted_iota(jnp.int32, (count, tail), 1)
            digit = jnp.where(lane == 0, index >> 7, jnp.where(lane == 1, index & 127, 0))
            unit_ref[:, width:] = digit.astype(F32).astype(BF)

    operands = [core, rows, *matrix] + ([] if partners is None else [partners])
    return call(
        kernel,
        (
            jax.ShapeDtypeStruct((count, width), F32),
            jax.ShapeDtypeStruct((count, width + tail), BF),
        ),
        in_specs=[pl.BlockSpec(memory_space=SMEM)]
        + [pl.BlockSpec(memory_space=VMEM)] * (len(operands) - 1),
        out_specs=[pl.BlockSpec(memory_space=VMEM)] * 2,
        flops=2 * count * width * width,
        moved=2 * width * width,
    )(*operands)


def project_back(core, pre, parts, matrix, out_dtype):
    count, width = pre.shape
    half = width // 2

    def kernel(core_ref, pre_ref, parts_ref, *refs):
        matrix_refs, out_ref = refs[:-1], refs[-1]
        upstream = parts_ref[0].astype(F32)
        for i in range(1, parts_ref.shape[0]):
            upstream += parts_ref[i].astype(F32)
        pre = pre_ref[...]
        inverse = lax.rsqrt(jnp.sum(pre * pre, axis=-1, keepdims=True) + EPSILON)
        along = jnp.sum(pre * upstream, axis=-1, keepdims=True)
        dpre = inverse * upstream - inverse**3 * pre * along
        if len(matrix) == 1:
            total = nn_dot(dpre.astype(BF), matrix_refs[0][...])
        else:
            first = core_ref[0] == 0
            low, high = dpre[:, :half], dpre[:, half:]
            mine = jnp.where(first, low, high).astype(BF)
            theirs = jnp.where(first, high, low).astype(BF)
            total = nn_dot(mine, matrix_refs[0][...]) + nn_dot(theirs, matrix_refs[1][...])
        out_ref[...] = total.astype(BF).astype(out_dtype)

    return call(
        kernel,
        jax.ShapeDtypeStruct((count, width), out_dtype),
        in_specs=[pl.BlockSpec(memory_space=SMEM)]
        + [pl.BlockSpec(memory_space=VMEM)] * (2 + len(matrix)),
        out_specs=pl.BlockSpec(memory_space=VMEM),
        flops=2 * count * width * width,
        moved=2 * width * width,
    )(core, pre, parts, *matrix)


def slopes(scalar_ref, texts, ids, lines, width):
    coolness, offset, scale = scalar_ref[0], scalar_ref[1], scalar_ref[2]
    logits = coolness * nt_dot(lines[:, :width], texts) + offset
    tail = lines[:, width:].astype(F32)
    match = tail[:, 0:1] * 128.0 + tail[:, 1:2] == ids
    steep = jnp.where(match, -scale, scale)
    slope = steep / (1.0 + jnp.exp(jnp.where(match, logits, -logits)))
    return slope.astype(BF)


def first_tile(scalars, pieces, text_ids, images):
    text_count = sum(piece.shape[0] for piece in pieces)
    image_count, width = images.shape[0], images.shape[1] - TAIL
    block = min(256, image_count)

    def kernel(scalar_ref, *refs):
        piece_refs = refs[: len(pieces)]
        ids_ref, images_ref, texts_ref, image_part_ref, total_ref = refs[len(pieces) :]
        start = 0
        for ref in piece_refs:
            texts_ref[start : start + ref.shape[0], :] = ref[...]
            start += ref.shape[0]
        ids = ids_ref[...]
        for i in range(image_count // block):
            rows = slice(i * block, (i + 1) * block)
            lines = images_ref[rows, :]
            weighted = slopes(scalar_ref, texts_ref[...], ids, lines, width)
            term = tn_dot(weighted, lines[:, :width])
            if i == 0:
                total_ref[...] = term
            else:
                total_ref[...] += term
            image_part_ref[rows, :] = nn_dot(weighted, texts_ref[...])

    return call(
        kernel,
        (
            jax.ShapeDtypeStruct((text_count, width), BF),
            jax.ShapeDtypeStruct((image_count, width), F32),
            jax.ShapeDtypeStruct((text_count, width), F32),
        ),
        in_specs=[pl.BlockSpec(memory_space=SMEM)]
        + [pl.BlockSpec(memory_space=VMEM)] * (2 + len(pieces)),
        out_specs=[pl.BlockSpec(memory_space=VMEM)] * 3,
        flops=6 * text_count * image_count * width,
        transcendentals=text_count * image_count,
        moved=2 * width * (text_count + 2 * image_count),
    )(scalars, *pieces, text_ids, images)


def second_tile(scalars, texts, text_ids, images, text_sum, cuts):
    text_count, width = texts.shape
    image_count = images.shape[0]
    block = min(256, image_count)

    def kernel(scalar_ref, texts_ref, ids_ref, images_ref, sum_ref, weighted_ref, *refs):
        out_refs, total_ref = refs[:-1], refs[-1]
        ids = ids_ref[...]
        for i in range(image_count // block):
            rows = slice(i * block, (i + 1) * block)
            lines = images_ref[rows, :]
            weighted = slopes(scalar_ref, texts_ref[...], ids, lines, width)
            weighted_ref[rows, :] = weighted
            term = tn_dot(weighted, lines[:, :width])
            if i == 0:
                total_ref[...] = sum_ref[...] + term
            else:
                total_ref[...] += term
        start = 0
        for ref in out_refs:
            ref[...] = total_ref[start : start + ref.shape[0], :].astype(ref.dtype)
            start += ref.shape[0]

    return call(
        kernel,
        (
            jax.ShapeDtypeStruct((image_count, text_count), BF),
            jax.ShapeDtypeStruct((cuts[0], width), F32),
            *(jax.ShapeDtypeStruct((size, width), BF) for size in cuts[1:]),
        ),
        in_specs=[pl.BlockSpec(memory_space=SMEM)] + [pl.BlockSpec(memory_space=VMEM)] * 4,
        out_specs=[pl.BlockSpec(memory_space=VMEM)] * (1 + len(cuts)),
        scratch_shapes=[pltpu.VMEM((text_count, width), F32)],
        flops=4 * text_count * image_count * width,
        transcendentals=text_count * image_count,
        moved=2 * width * (text_count + 2 * image_count),
    )(scalars, texts, text_ids, images, text_sum)


def image_terms(weighted, texts):
    image_count, text_count = weighted.shape
    width = texts.shape[1]

    def kernel(weighted_ref, texts_ref, out_ref):
        out_ref[...] = nn_dot(weighted_ref[...], texts_ref[...]).astype(BF)

    return call(
        kernel,
        jax.ShapeDtypeStruct((image_count, width), BF),
        in_specs=[pl.BlockSpec(memory_space=VMEM)] * 2,
        out_specs=pl.BlockSpec(memory_space=VMEM),
        flops=2 * text_count * image_count * width,
        moved=2 * width * (text_count + image_count),
    )(weighted, texts)


def add_up(total, parts):
    sizes = [len(part) for part in parts]

    def kernel(total_ref, *refs):
        out_ref = refs[-1]
        start = 0
        for cut in sorted(edges):
            rows = slice(start, cut)
            value = total_ref[rows, :]
            place = 0
            for size in sizes:
                base = 0
                for ref in refs[place : place + size]:
                    end = base + ref.shape[0]
                    if base <= start and cut <= end:
                        value = value + ref[start - base : cut - base, :].astype(F32)
                    base = end
                place += size
            out_ref[rows, :] = value.astype(BF)
            start = cut

    edges = set()
    for part in parts:
        end = 0
        for array in part:
            end += array.shape[0]
            edges.add(end)
    flat = [array for part in parts for array in part]
    return call(
        kernel,
        jax.ShapeDtypeStruct(total.shape, BF),
        in_specs=[pl.BlockSpec(memory_space=VMEM)] * (1 + len(flat)),
        out_specs=pl.BlockSpec(memory_space=VMEM),
        flops=total.size,
        moved=8 * total.size,
    )(total, *flat)


def to_all(values, axes, size):
    spread = jnp.broadcast_to(values[None], (size,) + values.shape)
    return lax.all_to_all(spread, axes, 0, 0, tiled=True)


def gather_matrix(piece):
    return to_all(piece, ("y_lo", "x"), 8).reshape(-1, piece.shape[1])


def shards(
    picture_tiles,
    query_key_product,
    pooling_exit_matrix,
    caption_embedding,
    caption_head_matrix,
    matching_caption_index,
    natural_inverse_coolness,
    score_offset,
    objective_adjoint,
):
    images, patches, width = picture_tiles.shape
    heads = query_key_product.shape[1]
    z_lo, y_hi, y_lo, x, core = (lax.axis_index(a) for a in ("z_lo", "y_hi", "y_lo", "x", "core"))
    place = core.astype(jnp.int32).reshape(1)
    count = caption_embedding.shape[0]

    exit_matrix = lax.all_gather(
        pooling_exit_matrix.T, ("core", "y_lo", "x"), axis=0, tiled=True
    )
    text_own = gather_matrix(caption_head_matrix.T)

    head_of = jnp.arange(width, dtype=jnp.int32) // (width // heads)
    spread = (head_of[None, :] == jnp.arange(heads, dtype=jnp.int32)[:, None]).astype(BF)
    gather = (head_of[:, None] == jnp.arange(heads, dtype=jnp.int32)[None, :]).astype(BF)
    tiles = picture_tiles.reshape(images * patches, width)
    attend, pooled = attention_forward(tiles, query_key_product, spread, patches)
    txt = (y_lo * NX + x) * NC + core
    kind = (z_lo + jnp.array([0, 1, 3, 2], jnp.int32)) % NZL
    source = (jnp.arange(NZH, dtype=jnp.int32)[None, :] * NZL + kind[:, None]).reshape(-1)
    first = (txt * (NZ * NYH) + source * NYH + y_hi) * count
    text_ids = first[:, None] + jnp.arange(count, dtype=jnp.int32)[None, :]
    text_ids = text_ids.astype(F32).reshape(1, -1)
    coolness = jnp.exp(natural_inverse_coolness[0])
    scalars = jnp.stack([coolness, score_offset[0], coolness * objective_adjoint[0]])
    partners = matching_caption_index.reshape(-1, 1)
    text_own, pooled, attend, text_ids, scalars, gather, partners = lax.optimization_barrier(
        (text_own, pooled, attend, text_ids, scalars, gather, partners)
    )

    text_matrix = text_own, swap_cores(text_own)
    text_pre, text_unit = project(place, caption_embedding, text_matrix)
    near = to_all(text_unit, "z_hi", NZH).reshape(-1, width)

    image_pre, image_unit = project(place, pooled, (exit_matrix,), partners)
    image_unit, near = lax.optimization_barrier((image_unit, near))
    own_images = to_all(image_unit, XY, 16).reshape(-1, width + TAIL)
    cut = near.shape[0] // 2
    pieces = [
        near,
        take_from(near, Z, 1, NZ),
        take_from(near, Z, -1, NZ),
        take_from(near[:cut], Z, 2, NZ),
        take_from(near[cut:], Z, -2, NZ),
    ]
    own_images, pieces = lax.optimization_barrier((own_images, pieces))
    other_images = swap_cores(own_images)

    texts, own_part, text_sum = first_tile(scalars, pieces, text_ids, own_images)
    weighted, mine, *away = second_tile(
        scalars, texts, text_ids, other_images, text_sum, [piece.shape[0] for piece in pieces]
    )
    away = [take_from(part, Z, -d, NZ) for part, d in zip(away, (1, -1, 2, -2))]
    other_part = swap_cores(image_terms(weighted, texts))
    chip_images = add_up(own_part, [[other_part]])
    image_parts = lax.all_to_all(chip_images.reshape(16, images, width), XY, 0, 0, tiled=True)
    chip_texts = add_up(mine, [[away[0]], [away[1]], away[2:]])
    image_parts, chip_texts = lax.optimization_barrier((image_parts, chip_texts))
    text_parts = lax.all_to_all(
        chip_texts.reshape(NZH, count, width), "z_hi", 0, 0, tiled=True
    )

    dpooled = project_back(place, image_pre, image_parts, (exit_matrix,), F32)
    d_patches = attention_backward(
        tiles, attend, dpooled, query_key_product.T, spread, gather, patches
    )
    text_pre, d_patches = lax.optimization_barrier((text_pre, d_patches))
    d_text = project_back(place, text_pre, text_parts, text_matrix, BF)
    return (d_patches.reshape(images, patches, width), d_text)


def solution(mesh):
    chips = Mesh(
        mesh.devices.reshape(NZH, NZL, NYH, NYL, NX, NC),
        ("z_hi", "z_lo", "y_hi", "y_lo", "x", "core"),
    )
    img, txt = ("z_hi", "z_lo", "y_hi"), ("y_lo", "x", "core")
    return jax.shard_map(
        shards,
        mesh=chips,
        in_specs=(
            P(img + txt, None, None),
            P(),
            P(None, txt),
            P(txt + img, None),
            P(None, txt),
            P(img + txt),
            P(),
            P(),
            P(),
        ),
        out_specs=(P(img + txt, None, None), P(txt + img, None)),
        check_vma=False,
    )
```

```python
import jax
import jax.numpy as jnp
from jax import lax
from jax.experimental import pallas as pl
from jax.experimental.pallas import tpu as pltpu
from jax.sharding import Mesh, PartitionSpec as P

EPSILON = 1e-06
INTERPRET = False
BF, F32 = jnp.bfloat16, jnp.float32
NZH, NZL, NYH, NYL, NX, NC = 4, 4, 2, 2, 4, 2
NZ = NZH * NZL
Z = ("z_hi", "z_lo")
XY = ("y_hi", "y_lo", "x")
TAIL = 128
TEXT_OFFSETS = (-4, 0, 4, 8, -3, 1, 5, 9, -5, -1, 3, 7, 2, 6, -6, -2)
VMEM = pltpu.VMEM
SMEM = pltpu.SMEM


def take_from(values, axis, distance, size):
    return lax.ppermute(values, axis, [((i + distance) % size, i) for i in range(size)])


def swap_cores(values):
    return lax.ppermute(values, "core", [(0, 1), (1, 0)])


def nt_dot(a, b):
    return lax.dot_general(a, b, (((1,), (1,)), ((), ())), preferred_element_type=F32)


def tn_dot(a, b):
    return lax.dot_general(a, b, (((0,), (0,)), ((), ())), preferred_element_type=F32)


def nn_dot(a, b):
    return jnp.dot(a, b, preferred_element_type=F32)


def call(kernel, out_shape, *, flops=0, transcendentals=0, moved=0, limit=16, **kw):
    return pl.pallas_call(
        kernel,
        out_shape=out_shape,
        compiler_params=pltpu.CompilerParams(vmem_limit_bytes=limit * 1024 * 1024),
        cost_estimate=pl.CostEstimate(
            flops=flops, transcendentals=transcendentals, bytes_accessed=moved
        ),
        interpret=INTERPRET,
        **kw,
    )


def attention_forward(tiles, query_key, spread, patches):
    rows, width = tiles.shape
    heads = query_key.shape[1]
    images = rows // patches
    step = min(8, images)

    def kernel(tile_ref, qk_ref, spread_ref, attend_ref, pooled_ref):
        tile = tile_ref[...]
        scores = nn_dot(tile, qk_ref[...]).reshape(step, patches, heads)
        top = jnp.max(scores, axis=1, keepdims=True)
        raised = jnp.exp(scores - top)
        attend = raised / jnp.sum(raised, axis=1, keepdims=True)
        attend = attend.reshape(step * patches, heads)
        attend_ref[...] = attend
        wide = nn_dot(attend.astype(BF), spread_ref[...])
        mixed = (wide * tile.astype(F32)).reshape(step, patches, width)
        pooled_ref[...] = jnp.sum(mixed, axis=1)

    return call(
        kernel,
        (
            jax.ShapeDtypeStruct((rows, heads), F32),
            jax.ShapeDtypeStruct((images, width), F32),
        ),
        grid=(images // step,),
        in_specs=[
            pl.BlockSpec((step * patches, width), lambda i: (i, 0)),
            pl.BlockSpec((width, heads), lambda i: (0, 0)),
            pl.BlockSpec((heads, width), lambda i: (0, 0)),
        ],
        out_specs=[
            pl.BlockSpec((step * patches, heads), lambda i: (i, 0)),
            pl.BlockSpec((step, width), lambda i: (i, 0)),
        ],
        flops=4 * rows * width * 128,
        moved=rows * width * 2,
    )(tiles, query_key, spread)


def attention_backward(tiles, attend, dpooled, query_key_t, spread, gather, patches):
    rows, width = tiles.shape
    heads = attend.shape[1]
    images = rows // patches
    step = min(8, images)

    def kernel(tile_ref, attend_ref, dpooled_ref, qkt_ref, spread_ref, gather_ref, out_ref):
        block = step * patches
        upstream = dpooled_ref[...]
        upstream = jnp.broadcast_to(upstream[:, None, :], (step, patches, width))
        upstream = upstream.reshape(block, width)
        product = tile_ref[...].astype(F32) * upstream
        high = product.astype(BF)
        low = (product - high.astype(F32)).astype(BF)
        dattend = nn_dot(high, gather_ref[...]) + nn_dot(low, gather_ref[...])
        attend = attend_ref[...]
        weighted = (attend * dattend).reshape(step, patches, heads)
        mean = jnp.broadcast_to(
            jnp.sum(weighted, axis=1, keepdims=True), (step, patches, heads)
        ).reshape(block, heads)
        dscores = attend * (dattend - mean)
        direct = nn_dot(attend.astype(BF), spread_ref[...]) * upstream
        through = nn_dot(dscores.astype(BF), qkt_ref[...])
        out_ref[...] = (direct + through).astype(BF)

    return call(
        kernel,
        jax.ShapeDtypeStruct((rows, width), BF),
        grid=(images // step,),
        in_specs=[
            pl.BlockSpec((step * patches, width), lambda i: (i, 0)),
            pl.BlockSpec((step * patches, heads), lambda i: (i, 0)),
            pl.BlockSpec((step, width), lambda i: (i, 0)),
            pl.BlockSpec((heads, width), lambda i: (0, 0)),
            pl.BlockSpec((heads, width), lambda i: (0, 0)),
            pl.BlockSpec((width, heads), lambda i: (0, 0)),
        ],
        out_specs=pl.BlockSpec((step * patches, width), lambda i: (i, 0)),
        flops=8 * rows * width * 128,
        moved=rows * width * 4,
    )(tiles, attend, dpooled, query_key_t, spread, gather)


def unit_rows(pre):
    inverse = lax.rsqrt(jnp.sum(pre * pre, axis=-1, keepdims=True) + EPSILON)
    return (pre * inverse).astype(BF)


def projected(core_ref, line, matrix_refs, pre_ref):
    if len(matrix_refs) == 1:
        return nt_dot(line, matrix_refs[0][...])
    half = matrix_refs[0].shape[0]
    first = core_ref[0] == 0
    mine, theirs = nt_dot(line, matrix_refs[0][...]), nt_dot(line, matrix_refs[1][...])
    pre_ref[:, :half] = jnp.where(first, mine, theirs)
    pre_ref[:, half:] = jnp.where(first, theirs, mine)
    return pre_ref[...]


def unit_texts(core, pieces, matrix):
    text_count = sum(piece.shape[0] for piece in pieces)
    width = pieces[0].shape[1]
    block = min(256, text_count)

    def kernel(core_ref, *refs):
        piece_refs, refs = refs[: len(pieces)], refs[len(pieces) :]
        matrix_refs, (texts_ref, pre_ref) = refs[: len(matrix)], refs[len(matrix) :]
        start = 0
        for ref in piece_refs:
            texts_ref[start : start + ref.shape[0], :] = ref[...]
            start += ref.shape[0]
        for i in range(text_count // block):
            rows = slice(i * block, (i + 1) * block)
            pre = projected(core_ref, texts_ref[rows, :], matrix_refs, pre_ref)
            texts_ref[rows, :] = unit_rows(pre)

    operands = [core, *pieces, *matrix]
    return call(
        kernel,
        jax.ShapeDtypeStruct((text_count, width), BF),
        in_specs=[pl.BlockSpec(memory_space=SMEM)]
        + [pl.BlockSpec(memory_space=VMEM)] * (len(operands) - 1),
        out_specs=pl.BlockSpec(memory_space=VMEM),
        scratch_shapes=[pltpu.VMEM((block, width), F32)],
        flops=2 * text_count * width * width,
        moved=2 * width * width,
    )(*operands)


def project_back(core, rows, parts, matrix, out_dtype):
    count, width = rows.shape
    half = width // 2

    def kernel(core_ref, rows_ref, parts_ref, *refs):
        matrix_refs, (out_ref, pre_ref) = refs[: len(matrix)], refs[len(matrix) :]
        pre = projected(core_ref, rows_ref[...].astype(BF), matrix_refs, pre_ref)
        upstream = parts_ref[0].astype(F32)
        for i in range(1, parts_ref.shape[0]):
            upstream += parts_ref[i].astype(F32)
        inverse = lax.rsqrt(jnp.sum(pre * pre, axis=-1, keepdims=True) + EPSILON)
        along = jnp.sum(pre * upstream, axis=-1, keepdims=True)
        dpre = inverse * upstream - inverse**3 * pre * along
        if len(matrix) == 1:
            total = nn_dot(dpre.astype(BF), matrix_refs[0][...])
        else:
            first = core_ref[0] == 0
            low, high = dpre[:, :half], dpre[:, half:]
            mine = jnp.where(first, low, high).astype(BF)
            theirs = jnp.where(first, high, low).astype(BF)
            total = nn_dot(mine, matrix_refs[0][...]) + nn_dot(theirs, matrix_refs[1][...])
        out_ref[...] = total.astype(BF).astype(out_dtype)

    return call(
        kernel,
        jax.ShapeDtypeStruct((count, width), out_dtype),
        in_specs=[pl.BlockSpec(memory_space=SMEM)]
        + [pl.BlockSpec(memory_space=VMEM)] * (2 + len(matrix)),
        out_specs=pl.BlockSpec(memory_space=VMEM),
        scratch_shapes=[pltpu.VMEM((count, width), F32)],
        flops=4 * count * width * width,
        moved=2 * width * width,
    )(core, rows, parts, *matrix)


def slopes(scalar_ref, texts, ids, units, tail):
    coolness, offset, scale = scalar_ref[0], scalar_ref[1], scalar_ref[2]
    logits = coolness * nt_dot(units, texts) + offset
    tail = tail.astype(F32)
    match = tail[:, 0:1] * 128.0 + tail[:, 1:2] == ids
    steep = jnp.where(match, -scale, scale)
    slope = steep / (1.0 + jnp.exp(jnp.where(match, logits, -logits)))
    return slope.astype(BF)


def first_tile(scalars, texts, text_ids, images, matrix):
    text_count, width = texts.shape
    image_count = images.shape[0]
    block = min(256, image_count)

    def kernel(scalar_ref, texts_ref, ids_ref, images_ref, matrix_ref, image_part_ref, total_ref):
        ids = ids_ref[...]
        for i in range(image_count // block):
            rows = slice(i * block, (i + 1) * block)
            units = unit_rows(nt_dot(images_ref[rows, :width], matrix_ref[...]))
            weighted = slopes(scalar_ref, texts_ref[...], ids, units, images_ref[rows, width:])
            term = tn_dot(weighted, units)
            if i == 0:
                total_ref[...] = term
            else:
                total_ref[...] += term
            image_part_ref[rows, :] = nn_dot(weighted, texts_ref[...])

    return call(
        kernel,
        (
            jax.ShapeDtypeStruct((image_count, width), F32),
            jax.ShapeDtypeStruct((text_count, width), F32),
        ),
        in_specs=[pl.BlockSpec(memory_space=SMEM)] + [pl.BlockSpec(memory_space=VMEM)] * 4,
        out_specs=[pl.BlockSpec(memory_space=VMEM)] * 2,
        flops=2 * image_count * width * (3 * text_count + width),
        transcendentals=text_count * image_count,
        moved=2 * width * (text_count + 2 * image_count),
    )(scalars, texts, text_ids, images, matrix)


def second_tile(scalars, texts, text_ids, images, matrix, text_sum, cuts):
    text_count, width = texts.shape
    image_count = images.shape[0]
    block = min(256, image_count)

    def kernel(
        scalar_ref, texts_ref, ids_ref, images_ref, matrix_ref, sum_ref, weighted_ref, *refs
    ):
        out_refs, total_ref = refs[:-1], refs[-1]
        ids = ids_ref[...]
        for i in range(image_count // block):
            rows = slice(i * block, (i + 1) * block)
            units = unit_rows(nt_dot(images_ref[rows, :width], matrix_ref[...]))
            weighted = slopes(scalar_ref, texts_ref[...], ids, units, images_ref[rows, width:])
            weighted_ref[rows, :] = weighted
            term = tn_dot(weighted, units)
            if i == 0:
                total_ref[...] = sum_ref[...] + term
            else:
                total_ref[...] += term
        start = 0
        for ref in out_refs:
            ref[...] = total_ref[start : start + ref.shape[0], :].astype(ref.dtype)
            start += ref.shape[0]

    return call(
        kernel,
        (
            jax.ShapeDtypeStruct((image_count, text_count), BF),
            jax.ShapeDtypeStruct((cuts[0], width), F32),
            *(jax.ShapeDtypeStruct((size, width), BF) for size in cuts[1:]),
        ),
        in_specs=[pl.BlockSpec(memory_space=SMEM)] + [pl.BlockSpec(memory_space=VMEM)] * 5,
        out_specs=[pl.BlockSpec(memory_space=VMEM)] * (1 + len(cuts)),
        scratch_shapes=[pltpu.VMEM((text_count, width), F32)],
        flops=2 * image_count * width * (2 * text_count + width),
        transcendentals=text_count * image_count,
        moved=2 * width * (text_count + 2 * image_count),
    )(scalars, texts, text_ids, images, matrix, text_sum)


def image_terms(weighted, texts):
    image_count, text_count = weighted.shape
    width = texts.shape[1]

    def kernel(weighted_ref, texts_ref, out_ref):
        out_ref[...] = nn_dot(weighted_ref[...], texts_ref[...]).astype(BF)

    return call(
        kernel,
        jax.ShapeDtypeStruct((image_count, width), BF),
        in_specs=[pl.BlockSpec(memory_space=VMEM)] * 2,
        out_specs=pl.BlockSpec(memory_space=VMEM),
        flops=2 * text_count * image_count * width,
        moved=2 * width * (text_count + image_count),
    )(weighted, texts)


def add_pair(total, part):
    def kernel(total_ref, part_ref, out_ref):
        out_ref[...] = (total_ref[...] + part_ref[...].astype(F32)).astype(BF)

    return call(
        kernel,
        jax.ShapeDtypeStruct(total.shape, BF),
        in_specs=[pl.BlockSpec(memory_space=VMEM)] * 2,
        out_specs=pl.BlockSpec(memory_space=VMEM),
        flops=total.size,
        moved=8 * total.size,
    )(total, part)


def add_texts(spot, total, near, far_low, far_high):
    rows, width = total.shape
    count = rows // NZH

    def kernel(spot_ref, total_ref, ahead_ref, behind_ref, low_ref, high_ref, out_ref, sum_ref):
        for i in range(NZH):
            piece = slice(i * count, (i + 1) * count)
            value = total_ref[piece, :] + ahead_ref[piece, :].astype(F32)
            value = value + behind_ref[piece, :].astype(F32)
            if i < 2:
                value = value + low_ref[piece, :].astype(F32)
            if 0 < i < 3:
                value = value + high_ref[(i - 1) * count : i * count, :].astype(F32)
            sum_ref[i] = value.astype(BF)
        for place in range(NZH):
            out_ref[place] = sum_ref[(place - spot_ref[0] + 1) & (NZH - 1)]

    return call(
        kernel,
        jax.ShapeDtypeStruct((NZH, count, width), BF),
        in_specs=[pl.BlockSpec(memory_space=SMEM)] + [pl.BlockSpec(memory_space=VMEM)] * 5,
        out_specs=pl.BlockSpec(memory_space=VMEM),
        scratch_shapes=[pltpu.VMEM((NZH, count, width), BF)],
        flops=3 * total.size,
        moved=8 * total.size,
    )(spot, total, *near, far_low, far_high)


def to_all(values, axes, size):
    spread = jnp.broadcast_to(values[None], (size,) + values.shape)
    return lax.all_to_all(spread, axes, 0, 0, tiled=True)


def gather_matrix(piece):
    return to_all(piece, ("y_lo", "x"), 8).reshape(-1, piece.shape[1])


def shards(
    picture_tiles,
    query_key_product,
    pooling_exit_matrix,
    caption_embedding,
    caption_head_matrix,
    matching_caption_index,
    natural_inverse_coolness,
    score_offset,
    objective_adjoint,
):
    images, patches, width = picture_tiles.shape
    heads = query_key_product.shape[1]
    z, y_hi, y_lo, x, core = (lax.axis_index(a) for a in (Z, "y_hi", "y_lo", "x", "core"))
    place = core.astype(jnp.int32).reshape(1)
    spot = lax.axis_index("z_hi").astype(jnp.int32).reshape(1)
    count = caption_embedding.shape[0]

    exit_matrix = lax.all_gather(
        pooling_exit_matrix.T, ("core", "y_lo", "x"), axis=0, tiled=True
    )
    text_own = gather_matrix(caption_head_matrix.T)

    near = [take_from(caption_embedding, Z, d, NZ) if d else caption_embedding for d in (-4, 0, 4, 8)]

    head_of = jnp.arange(width, dtype=jnp.int32) // (width // heads)
    spread = (head_of[None, :] == jnp.arange(heads, dtype=jnp.int32)[:, None]).astype(BF)
    gather = (head_of[:, None] == jnp.arange(heads, dtype=jnp.int32)[None, :]).astype(BF)
    tiles = picture_tiles.reshape(images * patches, width)
    attend, pooled = attention_forward(tiles, query_key_product, spread, patches)
    txt = (y_lo * NX + x) * NC + core
    source = (z + jnp.array(TEXT_OFFSETS, jnp.int32)) % NZ
    first = (txt * (NZ * NYH) + source * NYH + y_hi) * count
    text_ids = first[:, None] + jnp.arange(count, dtype=jnp.int32)[None, :]
    text_ids = text_ids.astype(F32).reshape(1, -1)
    coolness = jnp.exp(natural_inverse_coolness[0])
    scalars = jnp.stack([coolness, score_offset[0], coolness * objective_adjoint[0]])
    lane = jnp.arange(TAIL, dtype=jnp.int32)[None, :]
    index = matching_caption_index[:, None]
    digits = jnp.where(lane == 0, index >> 7, jnp.where(lane == 1, index & 127, 0))
    lines = jnp.concatenate([pooled.astype(BF), digits.astype(F32).astype(BF)], axis=1)

    text_own, lines, near, text_ids, scalars, gather = lax.optimization_barrier(
        (text_own, lines, near, text_ids, scalars, gather)
    )
    text_matrix = text_own, swap_cores(text_own)
    own_images = to_all(lines, XY, 16).reshape(-1, width + TAIL)
    near = jnp.concatenate(near, axis=0)
    pieces = [
        near,
        take_from(near, Z, 1, NZ),
        take_from(near, Z, -1, NZ),
        take_from(near[count : 3 * count], Z, 2, NZ),
        take_from(near[: 2 * count], Z, -2, NZ),
    ]
    own_images, pieces = lax.optimization_barrier((own_images, pieces))
    other_images = swap_cores(own_images)

    texts = unit_texts(place, pieces, text_matrix)
    own_part, text_sum = first_tile(scalars, texts, text_ids, own_images, exit_matrix)
    weighted, mine, *away = second_tile(
        scalars, texts, text_ids, other_images, exit_matrix, text_sum,
        [piece.shape[0] for piece in pieces],
    )
    away = [take_from(part, Z, -d, NZ) for part, d in zip(away, (1, -1, 2, -2))]
    other_part = swap_cores(image_terms(weighted, texts))
    chip_images = add_pair(own_part, other_part)
    image_parts = lax.all_to_all(chip_images.reshape(16, images, width), XY, 0, 0, tiled=True)
    chip_texts = add_texts(spot, mine, away[:2], away[3], away[2])
    image_parts, chip_texts = lax.optimization_barrier((image_parts, chip_texts))
    text_parts = lax.all_to_all(chip_texts, "z_hi", 0, 0, tiled=True)

    dpooled = project_back(place, pooled, image_parts, (exit_matrix,), F32)
    d_patches = attention_backward(
        tiles, attend, dpooled, query_key_product.T, spread, gather, patches
    )
    text_matrix, d_patches = lax.optimization_barrier((text_matrix, d_patches))
    d_text = project_back(place, caption_embedding, text_parts, text_matrix, BF)
    return (d_patches.reshape(images, patches, width), d_text)


def solution(mesh):
    chips = Mesh(
        mesh.devices.reshape(NZH, NZL, NYH, NYL, NX, NC),
        ("z_hi", "z_lo", "y_hi", "y_lo", "x", "core"),
    )
    img, txt = ("z_hi", "z_lo", "y_hi"), ("y_lo", "x", "core")
    return jax.shard_map(
        shards,
        mesh=chips,
        in_specs=(
            P(img + txt, None, None),
            P(),
            P(None, txt),
            P(txt + img, None),
            P(None, txt),
            P(img + txt),
            P(),
            P(),
            P(),
        ),
        out_specs=(P(img + txt, None, None), P(txt + img, None)),
        check_vma=False,
    )
```

```python
import jax
import jax.numpy as jnp
from jax import lax
from jax.experimental import pallas as pl
from jax.experimental.pallas import tpu as pltpu
from jax.sharding import Mesh, PartitionSpec as P

EPSILON = 1e-06
INTERPRET = False
BF, F32 = jnp.bfloat16, jnp.float32
NZH, NZL, NYH, NYL, NX, NC = 4, 4, 2, 2, 4, 2
NZ = NZH * NZL
Z = ("z_hi", "z_lo")
XY = ("y_hi", "y_lo", "x")
TAIL = 128
TEXT_OFFSETS = (-4, 0, 4, 8, -3, 1, 5, 9, -5, -1, 3, 7, 2, 6, -6, -2)
VMEM = pltpu.VMEM
SMEM = pltpu.SMEM


def take_from(values, axis, distance, size):
    return lax.ppermute(values, axis, [((i + distance) % size, i) for i in range(size)])


def swap_cores(values):
    return lax.ppermute(values, "core", [(0, 1), (1, 0)])


def nt_dot(a, b):
    return lax.dot_general(a, b, (((1,), (1,)), ((), ())), preferred_element_type=F32)


def tn_dot(a, b):
    return lax.dot_general(a, b, (((0,), (0,)), ((), ())), preferred_element_type=F32)


def nn_dot(a, b):
    return jnp.dot(a, b, preferred_element_type=F32)


def call(kernel, out_shape, *, flops=0, transcendentals=0, moved=0, limit=16, **kw):
    return pl.pallas_call(
        kernel,
        out_shape=out_shape,
        compiler_params=pltpu.CompilerParams(vmem_limit_bytes=limit * 1024 * 1024),
        cost_estimate=pl.CostEstimate(
            flops=flops, transcendentals=transcendentals, bytes_accessed=moved
        ),
        interpret=INTERPRET,
        **kw,
    )


def attention_forward(tiles, query_key, spread, patches):
    rows, width = tiles.shape
    heads = query_key.shape[1]
    images = rows // patches
    step = min(8, images)

    def kernel(tile_ref, qk_ref, spread_ref, attend_ref, pooled_ref):
        tile = tile_ref[...]
        scores = nn_dot(tile, qk_ref[...]).reshape(step, patches, heads)
        top = jnp.max(scores, axis=1, keepdims=True)
        raised = jnp.exp(scores - top)
        attend = raised / jnp.sum(raised, axis=1, keepdims=True)
        attend = attend.reshape(step * patches, heads)
        attend_ref[...] = attend
        wide = nn_dot(attend.astype(BF), spread_ref[...])
        mixed = (wide * tile.astype(F32)).reshape(step, patches, width)
        pooled_ref[...] = jnp.sum(mixed, axis=1)

    return call(
        kernel,
        (
            jax.ShapeDtypeStruct((rows, heads), F32),
            jax.ShapeDtypeStruct((images, width), F32),
        ),
        grid=(images // step,),
        in_specs=[
            pl.BlockSpec((step * patches, width), lambda i: (i, 0)),
            pl.BlockSpec((width, heads), lambda i: (0, 0)),
            pl.BlockSpec((heads, width), lambda i: (0, 0)),
        ],
        out_specs=[
            pl.BlockSpec((step * patches, heads), lambda i: (i, 0)),
            pl.BlockSpec((step, width), lambda i: (i, 0)),
        ],
        flops=4 * rows * width * 128,
        moved=rows * width * 2,
    )(tiles, query_key, spread)


def attention_backward(tiles, attend, dpooled, query_key_t, spread, gather, patches):
    rows, width = tiles.shape
    heads = attend.shape[1]
    images = rows // patches
    step = min(8, images)

    def kernel(tile_ref, attend_ref, dpooled_ref, qkt_ref, spread_ref, gather_ref, out_ref):
        block = step * patches
        upstream = dpooled_ref[...]
        upstream = jnp.broadcast_to(upstream[:, None, :], (step, patches, width))
        upstream = upstream.reshape(block, width)
        product = tile_ref[...].astype(F32) * upstream
        high = product.astype(BF)
        low = (product - high.astype(F32)).astype(BF)
        dattend = nn_dot(high, gather_ref[...]) + nn_dot(low, gather_ref[...])
        attend = attend_ref[...]
        weighted = (attend * dattend).reshape(step, patches, heads)
        mean = jnp.broadcast_to(
            jnp.sum(weighted, axis=1, keepdims=True), (step, patches, heads)
        ).reshape(block, heads)
        dscores = attend * (dattend - mean)
        direct = nn_dot(attend.astype(BF), spread_ref[...]) * upstream
        through = nn_dot(dscores.astype(BF), qkt_ref[...])
        out_ref[...] = (direct + through).astype(BF)

    return call(
        kernel,
        jax.ShapeDtypeStruct((rows, width), BF),
        grid=(images // step,),
        in_specs=[
            pl.BlockSpec((step * patches, width), lambda i: (i, 0)),
            pl.BlockSpec((step * patches, heads), lambda i: (i, 0)),
            pl.BlockSpec((step, width), lambda i: (i, 0)),
            pl.BlockSpec((heads, width), lambda i: (0, 0)),
            pl.BlockSpec((heads, width), lambda i: (0, 0)),
            pl.BlockSpec((width, heads), lambda i: (0, 0)),
        ],
        out_specs=pl.BlockSpec((step * patches, width), lambda i: (i, 0)),
        flops=8 * rows * width * 128,
        moved=rows * width * 4,
    )(tiles, attend, dpooled, query_key_t, spread, gather)


def unit_rows(pre):
    inverse = lax.rsqrt(jnp.sum(pre * pre, axis=-1, keepdims=True) + EPSILON)
    return (pre * inverse).astype(BF)


def projected(core_ref, line, matrix_refs, pre_ref):
    if len(matrix_refs) == 1:
        return nt_dot(line, matrix_refs[0][...])
    half = matrix_refs[0].shape[0]
    first = core_ref[0] == 0
    mine, theirs = nt_dot(line, matrix_refs[0][...]), nt_dot(line, matrix_refs[1][...])
    pre_ref[:, :half] = jnp.where(first, mine, theirs)
    pre_ref[:, half:] = jnp.where(first, theirs, mine)
    return pre_ref[...]


def unit_texts(core, pieces, matrix):
    text_count = sum(piece.shape[0] for piece in pieces)
    count = pieces[0].shape[0] // NZH
    width = pieces[0].shape[1]
    block = min(256, text_count)

    def kernel(core_ref, *refs):
        piece_refs, refs = refs[: len(pieces)], refs[len(pieces) :]
        matrix_refs, (texts_ref, own_ref, pre_ref, sems) = refs[: len(matrix)], refs[len(matrix) :]
        copies, start = [], 0
        for i, ref in enumerate(piece_refs):
            rows = pl.ds(start, ref.shape[0])
            copies.append(pltpu.make_async_copy(ref, texts_ref.at[rows], sems.at[i]))
            start += ref.shape[0]
        for copy in copies:
            copy.start()
        for copy in copies:
            copy.wait()
        for i in range(text_count // block):
            rows = slice(i * block, (i + 1) * block)
            pre = projected(core_ref, texts_ref[rows, :], matrix_refs, pre_ref)
            texts_ref[rows, :] = unit_rows(pre)
            if i == 0:
                own_ref[...] = pre[count : 2 * count]

    return call(
        kernel,
        (
            jax.ShapeDtypeStruct((text_count, width), BF),
            jax.ShapeDtypeStruct((count, width), F32),
        ),
        in_specs=[pl.BlockSpec(memory_space=SMEM)]
        + [pl.BlockSpec(memory_space=pl.ANY)] * len(pieces)
        + [pl.BlockSpec(memory_space=VMEM)] * len(matrix),
        out_specs=[pl.BlockSpec(memory_space=VMEM)] * 2,
        scratch_shapes=[
            pltpu.VMEM((block, width), F32),
            pltpu.SemaphoreType.DMA((len(pieces),)),
        ],
        flops=2 * text_count * width * width,
        moved=2 * width * width,
    )(core, *pieces, *matrix)


def project_back(core, rows, parts, matrix, out_dtype, before=False):
    count, width = rows.shape
    half = width // 2

    def kernel(core_ref, rows_ref, parts_ref, *refs):
        matrix_refs, (out_ref, pre_ref) = refs[: len(matrix)], refs[len(matrix) :]
        pre = rows_ref[...]
        if not before:
            pre = projected(core_ref, pre.astype(BF), matrix_refs, pre_ref)
        upstream = parts_ref[0].astype(F32)
        for i in range(1, parts_ref.shape[0]):
            upstream += parts_ref[i].astype(F32)
        inverse = lax.rsqrt(jnp.sum(pre * pre, axis=-1, keepdims=True) + EPSILON)
        along = jnp.sum(pre * upstream, axis=-1, keepdims=True)
        dpre = inverse * upstream - inverse**3 * pre * along
        if len(matrix) == 1:
            total = nn_dot(dpre.astype(BF), matrix_refs[0][...])
        else:
            first = core_ref[0] == 0
            low, high = dpre[:, :half], dpre[:, half:]
            mine = jnp.where(first, low, high).astype(BF)
            theirs = jnp.where(first, high, low).astype(BF)
            total = nn_dot(mine, matrix_refs[0][...]) + nn_dot(theirs, matrix_refs[1][...])
        out_ref[...] = total.astype(BF).astype(out_dtype)

    return call(
        kernel,
        jax.ShapeDtypeStruct((count, width), out_dtype),
        in_specs=[pl.BlockSpec(memory_space=SMEM)]
        + [pl.BlockSpec(memory_space=VMEM)] * (2 + len(matrix)),
        out_specs=pl.BlockSpec(memory_space=VMEM),
        scratch_shapes=[pltpu.VMEM((count, width), F32)],
        flops=4 * count * width * width,
        moved=2 * width * width,
    )(core, rows, parts, *matrix)


def slopes(scalar_ref, texts, ids, units, tail):
    coolness, offset, scale = scalar_ref[0], scalar_ref[1], scalar_ref[2]
    logits = coolness * nt_dot(units, texts) + offset
    tail = tail.astype(F32)
    match = tail[:, 0:1] * 128.0 + tail[:, 1:2] == ids
    steep = jnp.where(match, -scale, scale)
    slope = steep / (1.0 + jnp.exp(jnp.where(match, logits, -logits)))
    return slope.astype(BF)


def first_tile(core, scalars, texts, text_ids, images, matrix):
    text_count, width = texts.shape
    image_count = images.shape[0]
    block = min(256, image_count)

    def kernel(
        core_ref, scalar_ref, texts_ref, ids_ref, images_ref, mine_ref, theirs_ref,
        image_part_ref, total_ref, pre_ref,
    ):
        ids = ids_ref[...]
        for i in range(image_count // block):
            rows = slice(i * block, (i + 1) * block)
            line = images_ref[rows, :width]
            units = unit_rows(projected(core_ref, line, (mine_ref, theirs_ref), pre_ref))
            weighted = slopes(scalar_ref, texts_ref[...], ids, units, images_ref[rows, width:])
            term = tn_dot(weighted, units)
            if i == 0:
                total_ref[...] = term
            else:
                total_ref[...] += term
            image_part_ref[rows, :] = nn_dot(weighted, texts_ref[...])

    return call(
        kernel,
        (
            jax.ShapeDtypeStruct((image_count, width), F32),
            jax.ShapeDtypeStruct((text_count, width), F32),
        ),
        in_specs=[pl.BlockSpec(memory_space=SMEM)] * 2 + [pl.BlockSpec(memory_space=VMEM)] * 5,
        out_specs=[pl.BlockSpec(memory_space=VMEM)] * 2,
        scratch_shapes=[pltpu.VMEM((block, width), F32)],
        flops=2 * image_count * width * (3 * text_count + width),
        transcendentals=text_count * image_count,
        moved=2 * width * (text_count + 2 * image_count),
    )(core, scalars, texts, text_ids, images, *matrix)


def second_tile(core, scalars, texts, text_ids, images, matrix, text_sum, cuts):
    text_count, width = texts.shape
    image_count = images.shape[0]
    block = min(256, image_count)

    def kernel(
        core_ref, scalar_ref, texts_ref, ids_ref, images_ref, mine_ref, theirs_ref, sum_ref,
        weighted_ref, *refs,
    ):
        out_refs, (total_ref, pre_ref) = refs[:-2], refs[-2:]
        ids = ids_ref[...]
        for i in range(image_count // block):
            rows = slice(i * block, (i + 1) * block)
            line = images_ref[rows, :width]
            units = unit_rows(projected(core_ref, line, (mine_ref, theirs_ref), pre_ref))
            weighted = slopes(scalar_ref, texts_ref[...], ids, units, images_ref[rows, width:])
            weighted_ref[rows, :] = weighted
            term = tn_dot(weighted, units)
            if i == 0:
                total_ref[...] = sum_ref[...] + term
            else:
                total_ref[...] += term
        start = 0
        for ref in out_refs:
            ref[...] = total_ref[start : start + ref.shape[0], :].astype(ref.dtype)
            start += ref.shape[0]

    return call(
        kernel,
        (
            jax.ShapeDtypeStruct((image_count, text_count), BF),
            jax.ShapeDtypeStruct((cuts[0], width), F32),
            *(jax.ShapeDtypeStruct((size, width), BF) for size in cuts[1:]),
        ),
        in_specs=[pl.BlockSpec(memory_space=SMEM)] * 2 + [pl.BlockSpec(memory_space=VMEM)] * 6,
        out_specs=[pl.BlockSpec(memory_space=VMEM)] * (1 + len(cuts)),
        scratch_shapes=[pltpu.VMEM((text_count, width), F32), pltpu.VMEM((block, width), F32)],
        flops=2 * image_count * width * (2 * text_count + width),
        transcendentals=text_count * image_count,
        moved=2 * width * (text_count + 2 * image_count),
    )(core, scalars, texts, text_ids, images, *matrix, text_sum)


def image_terms(weighted, texts):
    image_count, text_count = weighted.shape
    width = texts.shape[1]

    def kernel(weighted_ref, texts_ref, out_ref):
        out_ref[...] = nn_dot(weighted_ref[...], texts_ref[...]).astype(BF)

    return call(
        kernel,
        jax.ShapeDtypeStruct((image_count, width), BF),
        in_specs=[pl.BlockSpec(memory_space=VMEM)] * 2,
        out_specs=pl.BlockSpec(memory_space=VMEM),
        flops=2 * text_count * image_count * width,
        moved=2 * width * (text_count + image_count),
    )(weighted, texts)


def add_pair(total, part):
    def kernel(total_ref, part_ref, out_ref):
        out_ref[...] = (total_ref[...] + part_ref[...].astype(F32)).astype(BF)

    return call(
        kernel,
        jax.ShapeDtypeStruct(total.shape, BF),
        in_specs=[pl.BlockSpec(memory_space=VMEM)] * 2,
        out_specs=pl.BlockSpec(memory_space=VMEM),
        flops=total.size,
        moved=8 * total.size,
    )(total, part)


def add_texts(spot, total, near, far_low, far_high):
    rows, width = total.shape
    count = rows // NZH

    def kernel(spot_ref, total_ref, ahead_ref, behind_ref, low_ref, high_ref, out_ref, sum_ref):
        for i in range(NZH):
            piece = slice(i * count, (i + 1) * count)
            value = total_ref[piece, :] + ahead_ref[piece, :].astype(F32)
            value = value + behind_ref[piece, :].astype(F32)
            if i < 2:
                value = value + low_ref[piece, :].astype(F32)
            if 0 < i < 3:
                value = value + high_ref[(i - 1) * count : i * count, :].astype(F32)
            sum_ref[i] = value.astype(BF)
        for place in range(NZH):
            out_ref[place] = sum_ref[(place - spot_ref[0] + 1) & (NZH - 1)]

    return call(
        kernel,
        jax.ShapeDtypeStruct((NZH, count, width), BF),
        in_specs=[pl.BlockSpec(memory_space=SMEM)] + [pl.BlockSpec(memory_space=VMEM)] * 5,
        out_specs=pl.BlockSpec(memory_space=VMEM),
        scratch_shapes=[pltpu.VMEM((NZH, count, width), BF)],
        flops=3 * total.size,
        moved=8 * total.size,
    )(spot, total, *near, far_low, far_high)


def to_all(values, axes, size):
    spread = jnp.broadcast_to(values[None], (size,) + values.shape)
    return lax.all_to_all(spread, axes, 0, 0, tiled=True)


def gather_matrix(piece):
    return lax.all_gather(piece, ("y_lo", "x"), axis=0, tiled=True)


def corner(*arrays):
    return sum(array[(0,) * (array.ndim - 1)][:1].astype(F32) for array in arrays)


def after(index, number):
    return index + (number != number).astype(jnp.int32)


def shards(
    picture_tiles,
    query_key_product,
    pooling_exit_matrix,
    caption_embedding,
    caption_head_matrix,
    matching_caption_index,
    natural_inverse_coolness,
    score_offset,
    objective_adjoint,
):
    images, patches, width = picture_tiles.shape
    heads = query_key_product.shape[1]
    z, y_hi, y_lo, x, core = (lax.axis_index(a) for a in (Z, "y_hi", "y_lo", "x", "core"))
    place = core.astype(jnp.int32).reshape(1)
    spot = lax.axis_index("z_hi").astype(jnp.int32).reshape(1)
    count = caption_embedding.shape[0]

    text_own = gather_matrix(caption_head_matrix.T)
    exit_own = gather_matrix(pooling_exit_matrix.T)

    captions = caption_embedding
    near = [take_from(captions, Z, d, NZ) if d else captions for d in (-4, 0, 4, 8)]
    head_of = jnp.arange(width, dtype=jnp.int32) // (width // heads)
    spread = (head_of[None, :] == jnp.arange(heads, dtype=jnp.int32)[:, None]).astype(BF)
    gather = (head_of[:, None] == jnp.arange(heads, dtype=jnp.int32)[None, :]).astype(BF)
    tiles = picture_tiles.reshape(images * patches, width)
    attend, pooled = attention_forward(tiles, query_key_product, spread, patches)
    txt = (y_lo * NX + x) * NC + core
    source = (z + jnp.array(TEXT_OFFSETS, jnp.int32)) % NZ
    first = (txt * (NZ * NYH) + source * NYH + y_hi) * count
    text_ids = first[:, None] + jnp.arange(count, dtype=jnp.int32)[None, :]
    text_ids = text_ids.astype(F32).reshape(1, -1)
    coolness = jnp.exp(natural_inverse_coolness[0])
    scalars = jnp.stack([coolness, score_offset[0], coolness * objective_adjoint[0]])
    lane = jnp.arange(TAIL, dtype=jnp.int32)[None, :]
    index = matching_caption_index[:, None]
    digits = jnp.where(lane == 0, index >> 7, jnp.where(lane == 1, index & 127, 0))
    lines = jnp.concatenate([pooled.astype(BF), digits.astype(F32).astype(BF)], axis=1)

    own_images = to_all(lines, XY, 16).reshape(-1, width + TAIL)
    near = jnp.concatenate(near, axis=0)
    pieces = [
        near,
        take_from(near, Z, 1, NZ),
        take_from(near, Z, -1, NZ),
        take_from(near[count : 3 * count], Z, 2, NZ),
        take_from(near[: 2 * count], Z, -2, NZ),
    ]
    text_matrix = text_own, swap_cores(text_own)
    held_exit, held_images, there = lax.optimization_barrier(
        (exit_own, own_images, corner(*pieces[1:]))
    )
    exit_matrix = exit_own, swap_cores(held_exit)
    other_images = swap_cores(held_images)

    texts, text_pre = unit_texts(after(place, there), pieces, text_matrix)
    own_part, text_sum = first_tile(
        place, scalars, texts, text_ids, own_images, exit_matrix
    )
    weighted, mine, *away = second_tile(
        place, scalars, texts, text_ids, other_images, exit_matrix, text_sum,
        [piece.shape[0] for piece in pieces],
    )
    away = [take_from(part, Z, -d, NZ) for part, d in zip(away, (1, -1, 2, -2))]
    other_part = swap_cores(image_terms(weighted, texts))
    chip_images = add_pair(own_part, other_part)
    image_parts = lax.all_to_all(chip_images.reshape(16, images, width), XY, 0, 0, tiled=True)
    chip_texts = add_texts(after(spot, corner(image_parts)), mine, away[:2], away[3], away[2])
    text_parts = lax.all_to_all(chip_texts, "z_hi", 0, 0, tiled=True)

    dpooled = project_back(place, pooled, image_parts, exit_matrix, F32)
    d_patches = attention_backward(
        tiles, attend, dpooled, query_key_product.T, spread, gather, patches
    )
    d_text = project_back(
        after(place, corner(d_patches)), text_pre, text_parts, text_matrix, BF, before=True)
    return (d_patches.reshape(images, patches, width), d_text)


def solution(mesh):
    chips = Mesh(
        mesh.devices.reshape(NZH, NZL, NYH, NYL, NX, NC),
        ("z_hi", "z_lo", "y_hi", "y_lo", "x", "core"),
    )
    img, txt = ("z_hi", "z_lo", "y_hi"), ("y_lo", "x", "core")
    return jax.shard_map(
        shards,
        mesh=chips,
        in_specs=(
            P(img + txt, None, None),
            P(),
            P(None, txt),
            P(txt + img, None),
            P(None, txt),
            P(img + txt),
            P(),
            P(),
            P(),
        ),
        out_specs=(P(img + txt, None, None), P(txt + img, None)),
        check_vma=False,
    )
```

```python
import jax
import jax.numpy as jnp
from jax import lax
from jax.experimental import pallas as pl
from jax.experimental.pallas import tpu as pltpu
from jax.sharding import Mesh, PartitionSpec as P

EPSILON = 1e-06
INTERPRET = False
BF, F32 = jnp.bfloat16, jnp.float32
NZH, NZL, NYH, NYL, NX, NC = 4, 4, 2, 2, 4, 2
NZ = NZH * NZL
Z = ("z_hi", "z_lo")
XY = ("y_hi", "y_lo", "x")
TAIL = 128
TEXT_OFFSETS = (-4, 0, 4, 8, -3, 1, 5, 9, -5, -1, 3, 7, 2, 6, -6, -2)
VMEM = pltpu.VMEM
SMEM = pltpu.SMEM


def take_from(values, axis, distance, size):
    return lax.ppermute(values, axis, [((i + distance) % size, i) for i in range(size)])


def swap_cores(values):
    return lax.ppermute(values, "core", [(0, 1), (1, 0)])


def nt_dot(a, b):
    return lax.dot_general(a, b, (((1,), (1,)), ((), ())), preferred_element_type=F32)


def tn_dot(a, b):
    return lax.dot_general(a, b, (((0,), (0,)), ((), ())), preferred_element_type=F32)


def nn_dot(a, b):
    return jnp.dot(a, b, preferred_element_type=F32)


def call(kernel, out_shape, *, flops=0, transcendentals=0, moved=0, limit=16, **kw):
    return pl.pallas_call(
        kernel,
        out_shape=out_shape,
        compiler_params=pltpu.CompilerParams(vmem_limit_bytes=limit * 1024 * 1024),
        cost_estimate=pl.CostEstimate(
            flops=flops, transcendentals=transcendentals, bytes_accessed=moved
        ),
        interpret=INTERPRET,
        **kw,
    )


def attention_forward(tiles, query_key, spread, patches):
    rows, width = tiles.shape
    heads = query_key.shape[1]
    images = rows // patches
    step = min(8, images)

    def kernel(tile_ref, qk_ref, spread_ref, attend_ref, pooled_ref):
        tile = tile_ref[...]
        scores = nn_dot(tile, qk_ref[...]).reshape(step, patches, heads)
        top = jnp.max(scores, axis=1, keepdims=True)
        raised = jnp.exp(scores - top)
        attend = raised / jnp.sum(raised, axis=1, keepdims=True)
        attend = attend.reshape(step * patches, heads)
        attend_ref[...] = attend
        wide = nn_dot(attend.astype(BF), spread_ref[...])
        mixed = (wide * tile.astype(F32)).reshape(step, patches, width)
        pooled_ref[...] = jnp.sum(mixed, axis=1)

    return call(
        kernel,
        (
            jax.ShapeDtypeStruct((rows, heads), F32),
            jax.ShapeDtypeStruct((images, width), F32),
        ),
        grid=(images // step,),
        in_specs=[
            pl.BlockSpec((step * patches, width), lambda i: (i, 0)),
            pl.BlockSpec((width, heads), lambda i: (0, 0)),
            pl.BlockSpec((heads, width), lambda i: (0, 0)),
        ],
        out_specs=[
            pl.BlockSpec((step * patches, heads), lambda i: (i, 0)),
            pl.BlockSpec((step, width), lambda i: (i, 0)),
        ],
        flops=4 * rows * width * 128,
        moved=rows * width * 2,
    )(tiles, query_key, spread)


def attention_backward(tiles, attend, dpooled, query_key_t, spread, gather, patches):
    rows, width = tiles.shape
    heads = attend.shape[1]
    images = rows // patches
    step = min(8, images)

    def kernel(tile_ref, attend_ref, dpooled_ref, qkt_ref, spread_ref, gather_ref, out_ref):
        block = step * patches
        upstream = dpooled_ref[...]
        upstream = jnp.broadcast_to(upstream[:, None, :], (step, patches, width))
        upstream = upstream.reshape(block, width)
        product = tile_ref[...].astype(F32) * upstream
        high = product.astype(BF)
        low = (product - high.astype(F32)).astype(BF)
        dattend = nn_dot(high, gather_ref[...]) + nn_dot(low, gather_ref[...])
        attend = attend_ref[...]
        weighted = (attend * dattend).reshape(step, patches, heads)
        mean = jnp.broadcast_to(
            jnp.sum(weighted, axis=1, keepdims=True), (step, patches, heads)
        ).reshape(block, heads)
        dscores = attend * (dattend - mean)
        direct = nn_dot(attend.astype(BF), spread_ref[...]) * upstream
        through = nn_dot(dscores.astype(BF), qkt_ref[...])
        out_ref[...] = (direct + through).astype(BF)

    return call(
        kernel,
        jax.ShapeDtypeStruct((rows, width), BF),
        grid=(images // step,),
        in_specs=[
            pl.BlockSpec((step * patches, width), lambda i: (i, 0)),
            pl.BlockSpec((step * patches, heads), lambda i: (i, 0)),
            pl.BlockSpec((step, width), lambda i: (i, 0)),
            pl.BlockSpec((heads, width), lambda i: (0, 0)),
            pl.BlockSpec((heads, width), lambda i: (0, 0)),
            pl.BlockSpec((width, heads), lambda i: (0, 0)),
        ],
        out_specs=pl.BlockSpec((step * patches, width), lambda i: (i, 0)),
        flops=8 * rows * width * 128,
        moved=rows * width * 4,
    )(tiles, attend, dpooled, query_key_t, spread, gather)


def unit_rows(pre):
    inverse = lax.rsqrt(jnp.sum(pre * pre, axis=-1, keepdims=True) + EPSILON)
    return (pre * inverse).astype(BF)


def projected(core_ref, line, matrix_refs, pre_ref):
    if len(matrix_refs) == 1:
        return nt_dot(line, matrix_refs[0][...])
    half = matrix_refs[0].shape[0]
    first = core_ref[0] == 0
    mine, theirs = nt_dot(line, matrix_refs[0][...]), nt_dot(line, matrix_refs[1][...])
    pre_ref[:, :half] = jnp.where(first, mine, theirs)
    pre_ref[:, half:] = jnp.where(first, theirs, mine)
    return pre_ref[...]


def unit_texts(core, pieces, matrix):
    text_count = sum(piece.shape[0] for piece in pieces)
    count = pieces[0].shape[0] // NZH
    width = pieces[0].shape[1]
    block = min(256, text_count)

    def kernel(core_ref, *refs):
        piece_refs, refs = refs[: len(pieces)], refs[len(pieces) :]
        matrix_refs, (texts_ref, own_ref, pre_ref, sems) = refs[: len(matrix)], refs[len(matrix) :]
        copies, start = [], 0
        for i, ref in enumerate(piece_refs):
            rows = pl.ds(start, ref.shape[0])
            copies.append(pltpu.make_async_copy(ref, texts_ref.at[rows], sems.at[i]))
            start += ref.shape[0]
        for copy in copies:
            copy.start()
        for copy in copies:
            copy.wait()
        for i in range(text_count // block):
            rows = slice(i * block, (i + 1) * block)
            pre = projected(core_ref, texts_ref[rows, :], matrix_refs, pre_ref)
            texts_ref[rows, :] = unit_rows(pre)
            if i == 0:
                own_ref[...] = pre[count : 2 * count]

    return call(
        kernel,
        (
            jax.ShapeDtypeStruct((text_count, width), BF),
            jax.ShapeDtypeStruct((count, width), F32),
        ),
        in_specs=[pl.BlockSpec(memory_space=SMEM)]
        + [pl.BlockSpec(memory_space=pl.ANY)] * len(pieces)
        + [pl.BlockSpec(memory_space=VMEM)] * len(matrix),
        out_specs=[pl.BlockSpec(memory_space=VMEM)] * 2,
        scratch_shapes=[
            pltpu.VMEM((block, width), F32),
            pltpu.SemaphoreType.DMA((len(pieces),)),
        ],
        flops=2 * text_count * width * width,
        moved=2 * width * width,
    )(core, *pieces, *matrix)


def project_back(core, rows, parts, matrix, out_dtype, before=False):
    count, width = rows.shape
    half = width // 2

    def kernel(core_ref, rows_ref, parts_ref, *refs):
        matrix_refs, (out_ref, pre_ref) = refs[: len(matrix)], refs[len(matrix) :]
        pre = rows_ref[...]
        if not before:
            pre = projected(core_ref, pre.astype(BF), matrix_refs, pre_ref)
        upstream = parts_ref[0].astype(F32)
        for i in range(1, parts_ref.shape[0]):
            upstream += parts_ref[i].astype(F32)
        inverse = lax.rsqrt(jnp.sum(pre * pre, axis=-1, keepdims=True) + EPSILON)
        along = jnp.sum(pre * upstream, axis=-1, keepdims=True)
        dpre = inverse * upstream - inverse**3 * pre * along
        if len(matrix) == 1:
            total = nn_dot(dpre.astype(BF), matrix_refs[0][...])
        else:
            first = core_ref[0] == 0
            low, high = dpre[:, :half], dpre[:, half:]
            mine = jnp.where(first, low, high).astype(BF)
            theirs = jnp.where(first, high, low).astype(BF)
            total = nn_dot(mine, matrix_refs[0][...]) + nn_dot(theirs, matrix_refs[1][...])
        out_ref[...] = total.astype(BF).astype(out_dtype)

    return call(
        kernel,
        jax.ShapeDtypeStruct((count, width), out_dtype),
        in_specs=[pl.BlockSpec(memory_space=SMEM)]
        + [pl.BlockSpec(memory_space=VMEM)] * (2 + len(matrix)),
        out_specs=pl.BlockSpec(memory_space=VMEM),
        scratch_shapes=[pltpu.VMEM((count, width), F32)],
        flops=4 * count * width * width,
        moved=2 * width * width,
    )(core, rows, parts, *matrix)


def slopes(scalar_ref, texts, ids, units, tail):
    coolness, offset, scale = scalar_ref[0], scalar_ref[1], scalar_ref[2]
    logits = coolness * nt_dot(units, texts) + offset
    tail = tail.astype(F32)
    match = tail[:, 0:1] * 128.0 + tail[:, 1:2] == ids
    steep = jnp.where(match, -scale, scale)
    slope = steep / (1.0 + jnp.exp(jnp.where(match, logits, -logits)))
    return slope.astype(BF)


def first_tile(core, scalars, texts, text_ids, images, matrix):
    text_count, width = texts.shape
    image_count = images.shape[0]
    block = min(256, image_count)

    def kernel(
        core_ref, scalar_ref, texts_ref, ids_ref, images_ref, mine_ref, theirs_ref,
        image_part_ref, total_ref, pre_ref,
    ):
        ids = ids_ref[...]
        for i in range(image_count // block):
            rows = slice(i * block, (i + 1) * block)
            line = images_ref[rows, :width]
            units = unit_rows(projected(core_ref, line, (mine_ref, theirs_ref), pre_ref))
            weighted = slopes(scalar_ref, texts_ref[...], ids, units, images_ref[rows, width:])
            term = tn_dot(weighted, units)
            if i == 0:
                total_ref[...] = term
            else:
                total_ref[...] += term
            image_part_ref[rows, :] = nn_dot(weighted, texts_ref[...])

    return call(
        kernel,
        (
            jax.ShapeDtypeStruct((image_count, width), F32),
            jax.ShapeDtypeStruct((text_count, width), F32),
        ),
        in_specs=[pl.BlockSpec(memory_space=SMEM)] * 2 + [pl.BlockSpec(memory_space=VMEM)] * 5,
        out_specs=[pl.BlockSpec(memory_space=VMEM)] * 2,
        scratch_shapes=[pltpu.VMEM((block, width), F32)],
        flops=2 * image_count * width * (3 * text_count + width),
        transcendentals=text_count * image_count,
        moved=2 * width * (text_count + 2 * image_count),
    )(core, scalars, texts, text_ids, images, *matrix)


def second_tile(core, scalars, texts, text_ids, images, matrix, text_sum, cuts):
    text_count, width = texts.shape
    image_count = images.shape[0]
    block = min(256, image_count)

    def kernel(
        core_ref, scalar_ref, texts_ref, ids_ref, images_ref, mine_ref, theirs_ref, sum_ref,
        weighted_ref, *refs,
    ):
        out_refs, (total_ref, pre_ref) = refs[:-2], refs[-2:]
        ids = ids_ref[...]
        for i in range(image_count // block):
            rows = slice(i * block, (i + 1) * block)
            line = images_ref[rows, :width]
            units = unit_rows(projected(core_ref, line, (mine_ref, theirs_ref), pre_ref))
            weighted = slopes(scalar_ref, texts_ref[...], ids, units, images_ref[rows, width:])
            weighted_ref[rows, :] = weighted
            term = tn_dot(weighted, units)
            if i == 0:
                total_ref[...] = sum_ref[...] + term
            else:
                total_ref[...] += term
        start = 0
        for ref in out_refs:
            ref[...] = total_ref[start : start + ref.shape[0], :].astype(ref.dtype)
            start += ref.shape[0]

    return call(
        kernel,
        (
            jax.ShapeDtypeStruct((image_count, text_count), BF),
            jax.ShapeDtypeStruct((cuts[0], width), F32),
            *(jax.ShapeDtypeStruct((size, width), BF) for size in cuts[1:]),
        ),
        in_specs=[pl.BlockSpec(memory_space=SMEM)] * 2 + [pl.BlockSpec(memory_space=VMEM)] * 6,
        out_specs=[pl.BlockSpec(memory_space=VMEM)] * (1 + len(cuts)),
        scratch_shapes=[pltpu.VMEM((text_count, width), F32), pltpu.VMEM((block, width), F32)],
        flops=2 * image_count * width * (2 * text_count + width),
        transcendentals=text_count * image_count,
        moved=2 * width * (text_count + 2 * image_count),
    )(core, scalars, texts, text_ids, images, *matrix, text_sum)


def image_terms(weighted, texts):
    image_count, text_count = weighted.shape
    width = texts.shape[1]

    def kernel(weighted_ref, texts_ref, out_ref):
        out_ref[...] = nn_dot(weighted_ref[...], texts_ref[...]).astype(BF)

    return call(
        kernel,
        jax.ShapeDtypeStruct((image_count, width), BF),
        in_specs=[pl.BlockSpec(memory_space=VMEM)] * 2,
        out_specs=pl.BlockSpec(memory_space=VMEM),
        flops=2 * text_count * image_count * width,
        moved=2 * width * (text_count + image_count),
    )(weighted, texts)


def add_pair(total, part):
    def kernel(total_ref, part_ref, out_ref):
        out_ref[...] = (total_ref[...] + part_ref[...].astype(F32)).astype(BF)

    return call(
        kernel,
        jax.ShapeDtypeStruct(total.shape, BF),
        in_specs=[pl.BlockSpec(memory_space=VMEM)] * 2,
        out_specs=pl.BlockSpec(memory_space=VMEM),
        flops=total.size,
        moved=8 * total.size,
    )(total, part)


def add_texts(spot, total, near, far_low, far_high):
    rows, width = total.shape
    count = rows // NZH

    def kernel(spot_ref, total_ref, ahead_ref, behind_ref, low_ref, high_ref, out_ref, sum_ref):
        for i in range(NZH):
            piece = slice(i * count, (i + 1) * count)
            value = total_ref[piece, :] + ahead_ref[piece, :].astype(F32)
            value = value + behind_ref[piece, :].astype(F32)
            if i < 2:
                value = value + low_ref[piece, :].astype(F32)
            if 0 < i < 3:
                value = value + high_ref[(i - 1) * count : i * count, :].astype(F32)
            sum_ref[i] = value.astype(BF)
        for place in range(NZH):
            out_ref[place] = sum_ref[(place - spot_ref[0] + 1) & (NZH - 1)]

    return call(
        kernel,
        jax.ShapeDtypeStruct((NZH, count, width), BF),
        in_specs=[pl.BlockSpec(memory_space=SMEM)] + [pl.BlockSpec(memory_space=VMEM)] * 5,
        out_specs=pl.BlockSpec(memory_space=VMEM),
        scratch_shapes=[pltpu.VMEM((NZH, count, width), BF)],
        flops=3 * total.size,
        moved=8 * total.size,
    )(spot, total, *near, far_low, far_high)


def to_all(values, axes, size):
    spread = jnp.broadcast_to(values[None], (size,) + values.shape)
    return lax.all_to_all(spread, axes, 0, 0, tiled=True)


def corner(*arrays):
    return sum(array[(0,) * (array.ndim - 1)][:1].astype(F32) for array in arrays)


def after(index, number):
    return index + (number != number).astype(jnp.int32)


def shards(
    picture_tiles,
    query_key_product,
    pooling_exit_matrix,
    caption_embedding,
    caption_head_matrix,
    matching_caption_index,
    natural_inverse_coolness,
    score_offset,
    objective_adjoint,
):
    images, patches, width = picture_tiles.shape
    heads = query_key_product.shape[1]
    z, y_hi, y_lo, x, core = (lax.axis_index(a) for a in (Z, "y_hi", "y_lo", "x", "core"))
    place = core.astype(jnp.int32).reshape(1)
    spot = lax.axis_index("z_hi").astype(jnp.int32).reshape(1)
    count = caption_embedding.shape[0]

    text_matrix = (
        lax.all_gather(caption_head_matrix.T, ("core", "y_lo", "x"), axis=0, tiled=True),
    )

    captions = caption_embedding
    near = [take_from(captions, Z, d, NZ) if d else captions for d in (-4, 0, 4, 8)]
    head_of = jnp.arange(width, dtype=jnp.int32) // (width // heads)
    spread = (head_of[None, :] == jnp.arange(heads, dtype=jnp.int32)[:, None]).astype(BF)
    gather = (head_of[:, None] == jnp.arange(heads, dtype=jnp.int32)[None, :]).astype(BF)
    tiles = picture_tiles.reshape(images * patches, width)
    attend, pooled = attention_forward(tiles, query_key_product, spread, patches)
    txt = (y_lo * NX + x) * NC + core
    source = (z + jnp.array(TEXT_OFFSETS, jnp.int32)) % NZ
    first = (txt * (NZ * NYH) + source * NYH + y_hi) * count
    text_ids = first[:, None] + jnp.arange(count, dtype=jnp.int32)[None, :]
    text_ids = text_ids.astype(F32).reshape(1, -1)
    coolness = jnp.exp(natural_inverse_coolness[0])
    scalars = jnp.stack([coolness, score_offset[0], coolness * objective_adjoint[0]])
    lane = jnp.arange(TAIL, dtype=jnp.int32)[None, :]
    index = matching_caption_index[:, None]
    digits = jnp.where(lane == 0, index >> 7, jnp.where(lane == 1, index & 127, 0))
    lines = jnp.concatenate([pooled.astype(BF), digits.astype(F32).astype(BF)], axis=1)

    own_images = to_all(lines, XY, 16).reshape(-1, width + TAIL)
    near = jnp.concatenate(near, axis=0)
    pieces = [
        near,
        take_from(near, Z, 1, NZ),
        take_from(near, Z, -1, NZ),
        take_from(near[count : 3 * count], Z, 2, NZ),
        take_from(near[: 2 * count], Z, -2, NZ),
    ]
    exit_piece, there = lax.optimization_barrier((pooling_exit_matrix.T, corner(own_images)))
    exit_own = to_all(exit_piece, ("y_lo", "x"), 8).reshape(-1, width)
    held_images, arrived = lax.optimization_barrier((own_images, corner(*pieces[1:])))
    exit_matrix = exit_own, swap_cores(exit_own)
    other_images = swap_cores(held_images)

    texts, text_pre = unit_texts(after(place, there + arrived), pieces, text_matrix)
    own_part, text_sum = first_tile(
        place, scalars, texts, text_ids, own_images, exit_matrix
    )
    weighted, mine, *away = second_tile(
        place, scalars, texts, text_ids, other_images, exit_matrix, text_sum,
        [piece.shape[0] for piece in pieces],
    )
    away = [take_from(part, Z, -d, NZ) for part, d in zip(away, (1, -1, 2, -2))]
    other_part = swap_cores(image_terms(weighted, texts))
    chip_images = add_pair(own_part, other_part)
    image_parts = lax.all_to_all(chip_images.reshape(16, images, width), XY, 0, 0, tiled=True)
    chip_texts = add_texts(after(spot, corner(image_parts)), mine, away[:2], away[3], away[2])
    text_parts = lax.all_to_all(chip_texts, "z_hi", 0, 0, tiled=True)

    dpooled = project_back(place, pooled, image_parts, exit_matrix, F32)
    d_patches = attention_backward(
        tiles, attend, dpooled, query_key_product.T, spread, gather, patches
    )
    d_text = project_back(
        after(place, corner(d_patches)), text_pre, text_parts, text_matrix, BF, before=True)
    return (d_patches.reshape(images, patches, width), d_text)


def solution(mesh):
    chips = Mesh(
        mesh.devices.reshape(NZH, NZL, NYH, NYL, NX, NC),
        ("z_hi", "z_lo", "y_hi", "y_lo", "x", "core"),
    )
    img, txt = ("z_hi", "z_lo", "y_hi"), ("y_lo", "x", "core")
    return jax.shard_map(
        shards,
        mesh=chips,
        in_specs=(
            P(img + txt, None, None),
            P(),
            P(None, txt),
            P(txt + img, None),
            P(None, txt),
            P(img + txt),
            P(),
            P(),
            P(),
        ),
        out_specs=(P(img + txt, None, None), P(txt + img, None)),
        check_vma=False,
    )
```

```python
import jax
import jax.numpy as jnp
from jax import lax
from jax.experimental import pallas as pl
from jax.experimental.pallas import tpu as pltpu
from jax.sharding import Mesh, PartitionSpec as P

EPSILON = 1e-06
INTERPRET = False
BF, F32 = jnp.bfloat16, jnp.float32
NZH, NZL, NYH, NYL, NX, NC = 4, 4, 2, 2, 4, 2
NZ = NZH * NZL
Z = ("z_hi", "z_lo")
XY = ("y_hi", "y_lo", "x")
TAIL = 128
VMEM = pltpu.VMEM
SMEM = pltpu.SMEM


def take_from(values, axis, distance, size):
    return lax.ppermute(values, axis, [((i + distance) % size, i) for i in range(size)])


def swap_cores(values):
    return lax.ppermute(values, "core", [(0, 1), (1, 0)])


def nt_dot(a, b):
    return lax.dot_general(a, b, (((1,), (1,)), ((), ())), preferred_element_type=F32)


def tn_dot(a, b):
    return lax.dot_general(a, b, (((0,), (0,)), ((), ())), preferred_element_type=F32)


def nn_dot(a, b):
    return jnp.dot(a, b, preferred_element_type=F32)


def call(kernel, out_shape, *, flops=0, transcendentals=0, moved=0, limit=16, **kw):
    return pl.pallas_call(
        kernel,
        out_shape=out_shape,
        compiler_params=pltpu.CompilerParams(vmem_limit_bytes=limit * 1024 * 1024),
        cost_estimate=pl.CostEstimate(
            flops=flops, transcendentals=transcendentals, bytes_accessed=moved
        ),
        interpret=INTERPRET,
        **kw,
    )


def attention_forward(tiles, query_key, spread, patches):
    rows, width = tiles.shape
    heads = query_key.shape[1]
    images = rows // patches
    step = min(8, images)

    def kernel(tile_ref, qk_ref, spread_ref, attend_ref, pooled_ref):
        tile = tile_ref[...]
        scores = nn_dot(tile, qk_ref[...]).reshape(step, patches, heads)
        top = jnp.max(scores, axis=1, keepdims=True)
        raised = jnp.exp(scores - top)
        attend = raised / jnp.sum(raised, axis=1, keepdims=True)
        attend = attend.reshape(step * patches, heads)
        attend_ref[...] = attend
        wide = nn_dot(attend.astype(BF), spread_ref[...])
        mixed = (wide * tile.astype(F32)).reshape(step, patches, width)
        pooled_ref[...] = jnp.sum(mixed, axis=1)

    return call(
        kernel,
        (
            jax.ShapeDtypeStruct((rows, heads), F32),
            jax.ShapeDtypeStruct((images, width), F32),
        ),
        grid=(images // step,),
        in_specs=[
            pl.BlockSpec((step * patches, width), lambda i: (i, 0)),
            pl.BlockSpec((width, heads), lambda i: (0, 0)),
            pl.BlockSpec((heads, width), lambda i: (0, 0)),
        ],
        out_specs=[
            pl.BlockSpec((step * patches, heads), lambda i: (i, 0)),
            pl.BlockSpec((step, width), lambda i: (i, 0)),
        ],
        flops=4 * rows * width * 128,
        moved=rows * width * 2,
    )(tiles, query_key, spread)


def attention_backward(tiles, attend, dpooled, query_key_t, spread, gather, patches):
    rows, width = tiles.shape
    heads = attend.shape[1]
    images = rows // patches
    step = min(8, images)

    def kernel(tile_ref, attend_ref, dpooled_ref, qkt_ref, spread_ref, gather_ref, out_ref):
        block = step * patches
        upstream = dpooled_ref[...]
        upstream = jnp.broadcast_to(upstream[:, None, :], (step, patches, width))
        upstream = upstream.reshape(block, width)
        product = tile_ref[...].astype(F32) * upstream
        high = product.astype(BF)
        low = (product - high.astype(F32)).astype(BF)
        dattend = nn_dot(high, gather_ref[...]) + nn_dot(low, gather_ref[...])
        attend = attend_ref[...]
        weighted = (attend * dattend).reshape(step, patches, heads)
        mean = jnp.broadcast_to(
            jnp.sum(weighted, axis=1, keepdims=True), (step, patches, heads)
        ).reshape(block, heads)
        dscores = attend * (dattend - mean)
        direct = nn_dot(attend.astype(BF), spread_ref[...]) * upstream
        through = nn_dot(dscores.astype(BF), qkt_ref[...])
        out_ref[...] = (direct + through).astype(BF)

    return call(
        kernel,
        jax.ShapeDtypeStruct((rows, width), BF),
        grid=(images // step,),
        in_specs=[
            pl.BlockSpec((step * patches, width), lambda i: (i, 0)),
            pl.BlockSpec((step * patches, heads), lambda i: (i, 0)),
            pl.BlockSpec((step, width), lambda i: (i, 0)),
            pl.BlockSpec((heads, width), lambda i: (0, 0)),
            pl.BlockSpec((heads, width), lambda i: (0, 0)),
            pl.BlockSpec((width, heads), lambda i: (0, 0)),
        ],
        out_specs=pl.BlockSpec((step * patches, width), lambda i: (i, 0)),
        flops=8 * rows * width * 128,
        moved=rows * width * 4,
    )(tiles, attend, dpooled, query_key_t, spread, gather)


def project(core, rows, matrix, partners=None):
    count, width = rows.shape
    half = width // 2
    tail = 0 if partners is None else TAIL

    def kernel(core_ref, rows_ref, *refs):
        matrix_refs, refs = refs[: len(matrix)], refs[len(matrix) :]
        pre_ref, unit_ref = refs[-2:]
        line = rows_ref[...].astype(BF)
        if len(matrix) == 1:
            pre = nt_dot(line, matrix_refs[0][...])
            pre_ref[...] = pre
        else:
            first = core_ref[0] == 0
            mine, theirs = nt_dot(line, matrix_refs[0][...]), nt_dot(line, matrix_refs[1][...])
            pre_ref[:, :half] = jnp.where(first, mine, theirs)
            pre_ref[:, half:] = jnp.where(first, theirs, mine)
            pre = pre_ref[...]
        inverse = lax.rsqrt(jnp.sum(pre * pre, axis=-1, keepdims=True) + EPSILON)
        unit_ref[:, :width] = (pre * inverse).astype(BF)
        if tail:
            index = refs[0][...]
            lane = lax.broadcasted_iota(jnp.int32, (count, tail), 1)
            digit = jnp.where(lane == 0, index >> 7, jnp.where(lane == 1, index & 127, 0))
            unit_ref[:, width:] = digit.astype(F32).astype(BF)

    operands = [core, rows, *matrix] + ([] if partners is None else [partners])
    return call(
        kernel,
        (
            jax.ShapeDtypeStruct((count, width), F32),
            jax.ShapeDtypeStruct((count, width + tail), BF),
        ),
        in_specs=[pl.BlockSpec(memory_space=SMEM)]
        + [pl.BlockSpec(memory_space=VMEM)] * (len(operands) - 1),
        out_specs=[pl.BlockSpec(memory_space=VMEM)] * 2,
        flops=2 * count * width * width,
        moved=2 * width * width,
    )(*operands)


def project_back(core, pre, parts, matrix, out_dtype):
    count, width = pre.shape
    half = width // 2

    def kernel(core_ref, pre_ref, parts_ref, *refs):
        matrix_refs, out_ref = refs[:-1], refs[-1]
        upstream = parts_ref[0].astype(F32)
        for i in range(1, parts_ref.shape[0]):
            upstream += parts_ref[i].astype(F32)
        pre = pre_ref[...]
        inverse = lax.rsqrt(jnp.sum(pre * pre, axis=-1, keepdims=True) + EPSILON)
        along = jnp.sum(pre * upstream, axis=-1, keepdims=True)
        dpre = inverse * upstream - inverse**3 * pre * along
        if len(matrix) == 1:
            total = nn_dot(dpre.astype(BF), matrix_refs[0][...])
        else:
            first = core_ref[0] == 0
            low, high = dpre[:, :half], dpre[:, half:]
            mine = jnp.where(first, low, high).astype(BF)
            theirs = jnp.where(first, high, low).astype(BF)
            total = nn_dot(mine, matrix_refs[0][...]) + nn_dot(theirs, matrix_refs[1][...])
        out_ref[...] = total.astype(BF).astype(out_dtype)

    return call(
        kernel,
        jax.ShapeDtypeStruct((count, width), out_dtype),
        in_specs=[pl.BlockSpec(memory_space=SMEM)]
        + [pl.BlockSpec(memory_space=VMEM)] * (2 + len(matrix)),
        out_specs=pl.BlockSpec(memory_space=VMEM),
        flops=2 * count * width * width,
        moved=2 * width * width,
    )(core, pre, parts, *matrix)


def slopes(scalar_ref, texts, ids, lines, width):
    coolness, offset, scale = scalar_ref[0], scalar_ref[1], scalar_ref[2]
    logits = coolness * nt_dot(lines[:, :width], texts) + offset
    tail = lines[:, width:].astype(F32)
    match = tail[:, 0:1] * 128.0 + tail[:, 1:2] == ids
    steep = jnp.where(match, -scale, scale)
    slope = steep / (1.0 + jnp.exp(jnp.where(match, logits, -logits)))
    return slope.astype(BF)


def first_tile(scalars, pieces, text_ids, images):
    text_count = sum(piece.shape[0] for piece in pieces)
    image_count, width = images.shape[0], images.shape[1] - TAIL
    block = min(256, image_count)

    def kernel(scalar_ref, *refs):
        piece_refs = refs[: len(pieces)]
        ids_ref, images_ref, texts_ref, image_part_ref, total_ref, sems = refs[len(pieces) :]
        copies, start = [], 0
        for i, ref in enumerate(piece_refs):
            rows = pl.ds(start, ref.shape[0])
            copies.append(pltpu.make_async_copy(ref, texts_ref.at[rows], sems.at[i]))
            start += ref.shape[0]
        for copy in copies:
            copy.start()
        for copy in copies:
            copy.wait()
        ids = ids_ref[...]
        for i in range(image_count // block):
            rows = slice(i * block, (i + 1) * block)
            lines = images_ref[rows, :]
            weighted = slopes(scalar_ref, texts_ref[...], ids, lines, width)
            term = tn_dot(weighted, lines[:, :width])
            if i == 0:
                total_ref[...] = term
            else:
                total_ref[...] += term
            image_part_ref[rows, :] = nn_dot(weighted, texts_ref[...])

    return call(
        kernel,
        (
            jax.ShapeDtypeStruct((text_count, width), BF),
            jax.ShapeDtypeStruct((image_count, width), F32),
            jax.ShapeDtypeStruct((text_count, width), F32),
        ),
        in_specs=[pl.BlockSpec(memory_space=SMEM)]
        + [pl.BlockSpec(memory_space=pl.ANY)] * len(pieces)
        + [pl.BlockSpec(memory_space=VMEM)] * 2,
        out_specs=[pl.BlockSpec(memory_space=VMEM)] * 3,
        scratch_shapes=[pltpu.SemaphoreType.DMA((len(pieces),))],
        flops=6 * text_count * image_count * width,
        transcendentals=text_count * image_count,
        moved=2 * width * (text_count + 2 * image_count),
    )(scalars, *pieces, text_ids, images)


def second_tile(scalars, texts, text_ids, images, text_sum, cuts):
    text_count, width = texts.shape
    image_count = images.shape[0]
    block = min(256, image_count)

    def kernel(scalar_ref, texts_ref, ids_ref, images_ref, sum_ref, weighted_ref, *refs):
        out_refs, total_ref = refs[:-1], refs[-1]
        ids = ids_ref[...]
        for i in range(image_count // block):
            rows = slice(i * block, (i + 1) * block)
            lines = images_ref[rows, :]
            weighted = slopes(scalar_ref, texts_ref[...], ids, lines, width)
            weighted_ref[rows, :] = weighted
            term = tn_dot(weighted, lines[:, :width])
            if i == 0:
                total_ref[...] = sum_ref[...] + term
            else:
                total_ref[...] += term
        start = 0
        for ref in out_refs:
            ref[...] = total_ref[start : start + ref.shape[0], :].astype(ref.dtype)
            start += ref.shape[0]

    return call(
        kernel,
        (
            jax.ShapeDtypeStruct((image_count, text_count), BF),
            jax.ShapeDtypeStruct((cuts[0], width), F32),
            *(jax.ShapeDtypeStruct((size, width), BF) for size in cuts[1:]),
        ),
        in_specs=[pl.BlockSpec(memory_space=SMEM)] + [pl.BlockSpec(memory_space=VMEM)] * 4,
        out_specs=[pl.BlockSpec(memory_space=VMEM)] * (1 + len(cuts)),
        scratch_shapes=[pltpu.VMEM((text_count, width), F32)],
        flops=4 * text_count * image_count * width,
        transcendentals=text_count * image_count,
        moved=2 * width * (text_count + 2 * image_count),
    )(scalars, texts, text_ids, images, text_sum)


def image_terms(weighted, texts):
    image_count, text_count = weighted.shape
    width = texts.shape[1]

    def kernel(weighted_ref, texts_ref, out_ref):
        out_ref[...] = nn_dot(weighted_ref[...], texts_ref[...]).astype(BF)

    return call(
        kernel,
        jax.ShapeDtypeStruct((image_count, width), BF),
        in_specs=[pl.BlockSpec(memory_space=VMEM)] * 2,
        out_specs=pl.BlockSpec(memory_space=VMEM),
        flops=2 * text_count * image_count * width,
        moved=2 * width * (text_count + image_count),
    )(weighted, texts)


def add_up(total, parts):
    sizes = [len(part) for part in parts]

    def kernel(total_ref, *refs):
        out_ref = refs[-1]
        start = 0
        for cut in sorted(edges):
            rows = slice(start, cut)
            value = total_ref[rows, :]
            place = 0
            for size in sizes:
                base = 0
                for ref in refs[place : place + size]:
                    end = base + ref.shape[0]
                    if base <= start and cut <= end:
                        value = value + ref[start - base : cut - base, :].astype(F32)
                    base = end
                place += size
            out_ref[rows, :] = value.astype(BF)
            start = cut

    edges = set()
    for part in parts:
        end = 0
        for array in part:
            end += array.shape[0]
            edges.add(end)
    flat = [array for part in parts for array in part]
    return call(
        kernel,
        jax.ShapeDtypeStruct(total.shape, BF),
        in_specs=[pl.BlockSpec(memory_space=VMEM)] * (1 + len(flat)),
        out_specs=pl.BlockSpec(memory_space=VMEM),
        flops=total.size,
        moved=8 * total.size,
    )(total, *flat)


def to_all(values, axes, size):
    spread = jnp.broadcast_to(values[None], (size,) + values.shape)
    return lax.all_to_all(spread, axes, 0, 0, tiled=True)


def gather_matrix(piece):
    return to_all(piece, ("y_lo", "x"), 8).reshape(-1, piece.shape[1])


def shards(
    picture_tiles,
    query_key_product,
    pooling_exit_matrix,
    caption_embedding,
    caption_head_matrix,
    matching_caption_index,
    natural_inverse_coolness,
    score_offset,
    objective_adjoint,
):
    images, patches, width = picture_tiles.shape
    heads = query_key_product.shape[1]
    z_lo, y_hi, y_lo, x, core = (lax.axis_index(a) for a in ("z_lo", "y_hi", "y_lo", "x", "core"))
    place = core.astype(jnp.int32).reshape(1)
    count = caption_embedding.shape[0]

    exit_matrix = lax.all_gather(
        pooling_exit_matrix.T, ("core", "y_lo", "x"), axis=0, tiled=True
    )
    text_own = gather_matrix(caption_head_matrix.T)

    head_of = jnp.arange(width, dtype=jnp.int32) // (width // heads)
    spread = (head_of[None, :] == jnp.arange(heads, dtype=jnp.int32)[:, None]).astype(BF)
    gather = (head_of[:, None] == jnp.arange(heads, dtype=jnp.int32)[None, :]).astype(BF)
    tiles = picture_tiles.reshape(images * patches, width)
    attend, pooled = attention_forward(tiles, query_key_product, spread, patches)
    txt = (y_lo * NX + x) * NC + core
    kind = (z_lo + jnp.array([0, 1, 3, 2], jnp.int32)) % NZL
    source = (jnp.arange(NZH, dtype=jnp.int32)[None, :] * NZL + kind[:, None]).reshape(-1)
    first = (txt * (NZ * NYH) + source * NYH + y_hi) * count
    text_ids = first[:, None] + jnp.arange(count, dtype=jnp.int32)[None, :]
    text_ids = text_ids.astype(F32).reshape(1, -1)
    coolness = jnp.exp(natural_inverse_coolness[0])
    scalars = jnp.stack([coolness, score_offset[0], coolness * objective_adjoint[0]])
    partners = matching_caption_index.reshape(-1, 1)
    text_own, pooled, attend, text_ids, scalars, gather, partners = lax.optimization_barrier(
        (text_own, pooled, attend, text_ids, scalars, gather, partners)
    )

    text_matrix = text_own, swap_cores(text_own)
    text_pre, text_unit = project(place, caption_embedding, text_matrix)
    near = to_all(text_unit, "z_hi", NZH).reshape(-1, width)

    image_pre, image_unit = project(place, pooled, (exit_matrix,), partners)
    image_unit, near = lax.optimization_barrier((image_unit, near))
    own_images = to_all(image_unit, XY, 16).reshape(-1, width + TAIL)
    cut = near.shape[0] // 2
    pieces = [
        near,
        take_from(near, Z, 1, NZ),
        take_from(near, Z, -1, NZ),
        take_from(near[:cut], Z, 2, NZ),
        take_from(near[cut:], Z, -2, NZ),
    ]
    there = sum(piece[0, :1].astype(F32) for piece in pieces[1:])
    held_images, there = lax.optimization_barrier((own_images, there))
    other_images = swap_cores(held_images)
    first_scalars = scalars + (there != there).astype(F32)

    texts, own_part, text_sum = first_tile(first_scalars, pieces, text_ids, own_images)
    weighted, mine, *away = second_tile(
        scalars, texts, text_ids, other_images, text_sum, [piece.shape[0] for piece in pieces]
    )
    away = [take_from(part, Z, -d, NZ) for part, d in zip(away, (1, -1, 2, -2))]
    other_part = swap_cores(image_terms(weighted, texts))
    chip_images = add_up(own_part, [[other_part]])
    image_parts = lax.all_to_all(chip_images.reshape(16, images, width), XY, 0, 0, tiled=True)
    chip_texts = add_up(mine, [[away[0]], [away[1]], away[2:]])
    image_parts, chip_texts = lax.optimization_barrier((image_parts, chip_texts))
    text_parts = lax.all_to_all(
        chip_texts.reshape(NZH, count, width), "z_hi", 0, 0, tiled=True
    )

    dpooled = project_back(place, image_pre, image_parts, (exit_matrix,), F32)
    d_patches = attention_backward(
        tiles, attend, dpooled, query_key_product.T, spread, gather, patches
    )
    text_pre, d_patches = lax.optimization_barrier((text_pre, d_patches))
    d_text = project_back(place, text_pre, text_parts, text_matrix, BF)
    return (d_patches.reshape(images, patches, width), d_text)


def solution(mesh):
    chips = Mesh(
        mesh.devices.reshape(NZH, NZL, NYH, NYL, NX, NC),
        ("z_hi", "z_lo", "y_hi", "y_lo", "x", "core"),
    )
    img, txt = ("z_hi", "z_lo", "y_hi"), ("y_lo", "x", "core")
    return jax.shard_map(
        shards,
        mesh=chips,
        in_specs=(
            P(img + txt, None, None),
            P(),
            P(None, txt),
            P(txt + img, None),
            P(None, txt),
            P(img + txt),
            P(),
            P(),
            P(),
        ),
        out_specs=(P(img + txt, None, None), P(txt + img, None)),
        check_vma=False,
    )
```
